128 devices in a mesh: tp: 2 (over core), grp: 32 (over z, y, x_lo), rep: 2 (over x_hi).
Axes of the slice: x: 4 (x_hi: 2, x_lo: 2; x = x_hi * 2 + x_lo), y: 4, z: 4, core: 2. Of those that a mesh axis runs over, the one named last changes fastest.
Arguments:
- tokens: bfloat16 [8192, 4096], P(('rep', 'tp', 'grp')), parts along dimension 0, may hold values from -6 to 6
- qkv_weight: bfloat16 [4096, 5120], P(None, ('tp', 'grp')), may hold values from -0.09375 to 0.09375
- qkv_bias: bfloat16 [5120], replicated, may hold values from -3 to 3
- cache: bfloat16 [512, 1024, 1024], P(('rep', 'tp', 'grp')), parts along dimension 0, may hold values from -80 to 80
- lengths: int32 [512], P('rep'), parts along dimension 0, may hold values from 128 to 1024, as said below
- slot_stream: int32 [512], P('rep'), parts along dimension 0, may hold values from 0 to 255, each once
Outputs:
- attended: bfloat16 [8192, 4096], P(('rep', 'tp', 'grp')), parts along dimension 0
The draws below stay inside these ranges and needn't reach their ends.
There are 2 independent parts, one for each index of `rep`. The reference program is written for one: setup_inputs(seed, part) draws one part's arguments, and reference() takes and returns one part's arrays. A program takes and returns all parts, laid end to end along the dimension named above; an argument that names none is the same for every part. Nothing has to cross between parts.
Inputs may be any that keep to these rules, and one draw needn't show every extreme that they name: `lengths`: cache length of each stream; some stream has exactly 1024 and some exactly 128. `slot_stream`: each stream appears in exactly one slot.
All inputs are finite; a program needn't handle non-finite values.
Results may differ from the reference program's by a relative error of at most 0.004.
The reference program's roundings to bfloat16 on the way count: a program that leaves them out, or rounds other values in their place, can miss the bound.
Values may be sent and summed in bfloat16 or wider, within the bound.
No kernel may reach another device: no remote copies, remote signals or barrier semaphores. Data moves between devices by JAX's collectives and lax.ppermute only.
A program may use at most 128 MiB of HBM per device.

```python
import jax
import jax.numpy as jnp
from jax import lax

D = 4096
HD = 128
HQ = 32
KVH = 4
STRETCH = 16
CAP = 1024
GROUP = 8
STREAMS = 256
ROWS = 4096
QKV_COLS = 5120


def draw_cache(key, part):
    key_base = jax.random.fold_in(key, 11)
    column = jnp.arange(2 * KVH * HD, dtype=jnp.int32)
    base_draw = jax.random.normal(key_base, (STREAMS, CAP, 2 * KVH * HD), jnp.float32)
    boost_factor = jnp.ones((STREAMS, CAP, 1), jnp.float32)
    column_scale = jnp.where(column[None, None, :] < KVH * HD, 3.0 * boost_factor, 1.0)
    return (base_draw * column_scale).astype(jnp.bfloat16)


def draw_lengths(key, part):
    key_values = jax.random.fold_in(key, 21)
    key_longest = jax.random.fold_in(key, 22)
    values = jax.random.randint(key_values, (STREAMS,), CAP // 8, CAP + 1)
    longest = jax.random.randint(key_longest, (), 0, STREAMS)
    shortest = (longest + 1) % STREAMS
    values = values.at[longest].set(CAP)
    values = values.at[shortest].set(CAP // 8)
    return values.astype(jnp.int32)


def block_levels(own_key, dims, pieces, smallest, high):
    level = 1.0
    for axis_at, parts in pieces:
        heights = jax.random.uniform(jax.random.fold_in(jax.random.fold_in(own_key, 6), axis_at), (parts,), jnp.float32, smallest / len(pieces), high / len(pieces))
        level = level * jnp.repeat(jnp.exp(heights), dims[axis_at] // parts).reshape((-1,) + (1,) * (len(dims) - 1 - axis_at))
    return level


def bell_draw(rng, dims, scale, reach, split=(), held_as=jnp.bfloat16):
    gain = block_levels(rng, dims, split, -0.22, 0.18) if split else 1.0
    drawn = jax.random.normal(rng, dims, jnp.float32) * scale * gain
    return jnp.minimum(jnp.maximum(drawn, -reach), reach).astype(held_as)


def setup_inputs(seed: int = 0, part: int = 0) -> dict:
    key_of = jax.random.split(jax.random.key(seed), 7)
    own_keys = jax.random.split(jax.random.fold_in(key_of[6], part), 7)
    return {
        "tokens": bell_draw(own_keys[0], (ROWS, D), 1.0, 6.0, ((0, 64),)),
        "qkv_weight": bell_draw(key_of[1], (D, QKV_COLS), D ** -0.5, 0.09375, ((1, 64),)),
        "qkv_bias": bell_draw(key_of[2], (QKV_COLS,), 0.5, 3.0),
        "cache": draw_cache(jax.random.fold_in(jax.random.fold_in(key_of[6], part), 71), part),
        "lengths": draw_lengths(jax.random.fold_in(jax.random.fold_in(key_of[6], part), 71), part),
        "slot_stream": jax.random.permutation(own_keys[5], STREAMS).astype(jnp.int32),
    }


ROPE_THETA = 1000000.0


def rotate(vectors, positions):
    half_width = vectors.shape[-1] // 2
    frequency = ROPE_THETA ** (-(jnp.arange(half_width, dtype=jnp.float32) * 2.0) / vectors.shape[-1])
    angles = positions.astype(jnp.float32)[:, None] * frequency[None, :]
    cosine = jnp.cos(angles)[:, None, :]
    sine_part = jnp.sin(angles)[:, None, :]
    front_half = vectors[..., :half_width]
    back_half = vectors[..., half_width:]
    return jnp.concatenate([front_half * cosine - back_half * sine_part, back_half * cosine + front_half * sine_part], axis=-1)


def rounded(values):
    return lax.optimization_barrier(values.astype(jnp.bfloat16)).astype(jnp.float32)


def reference(tokens, qkv_weight, qkv_bias, cache, lengths, slot_stream):
    query_width = HQ * HD
    kv_width = KVH * HD
    projected_qkv = (jnp.dot(tokens, qkv_weight, preferred_element_type=jnp.float32) + qkv_bias.astype(jnp.float32)[None, :]).astype(jnp.bfloat16)
    projected_qkv = projected_qkv.reshape(STREAMS, STRETCH, QKV_COLS)
    token_index = jnp.arange(STRETCH, dtype=jnp.int32)
    key_index = jnp.arange(CAP + STRETCH, dtype=jnp.int32)
    score_scale = HD ** -0.5

    def one_slot(inputs):
        slot_cache, token_slab, stream = inputs
        length = lax.dynamic_index_in_dim(lengths, stream, 0, keepdims=False)
        token_block = token_slab.astype(jnp.float32)
        positions = length + token_index
        queries = rounded(rotate(token_block[:, :query_width].reshape(STRETCH, HQ, HD), positions)).reshape(STRETCH, KVH, GROUP, HD)
        new_keys = rounded(rotate(token_block[:, query_width:query_width + kv_width].reshape(STRETCH, KVH, HD), positions))
        new_values = token_block[:, query_width + kv_width:].reshape(STRETCH, KVH, HD)
        cache_float = slot_cache.astype(jnp.float32)
        key_all = jnp.concatenate([cache_float[:, :kv_width].reshape(CAP, KVH, HD), new_keys], axis=0)
        value_all = jnp.concatenate([cache_float[:, kv_width:].reshape(CAP, KVH, HD), new_values], axis=0)
        scores = jnp.einsum("ckgd,jkd->ckgj", queries, key_all, precision=lax.Precision.HIGHEST) * score_scale
        allowed = jnp.where(key_index[None, :] < CAP, key_index[None, :] < length, key_index[None, :] - CAP <= token_index[:, None])
        scores = jnp.where(allowed[:, None, None, :], scores, -jnp.inf)
        row_max = jnp.max(scores, axis=-1, keepdims=True)
        exponent = jnp.exp(scores - row_max)
        row_total = jnp.sum(exponent, axis=-1, keepdims=True)
        result = jnp.einsum("ckgj,jkd->ckgd", rounded(exponent), value_all, precision=lax.Precision.HIGHEST) / row_total
        return result.reshape(STRETCH, HQ * HD).astype(jnp.bfloat16)

    attended = lax.map(one_slot, (cache, projected_qkv, slot_stream))
    return attended.reshape(ROWS, HQ * HD)
```

```python
import functools

import jax
import jax.numpy as jnp
from jax import lax
from jax.experimental import pallas as pl
from jax.experimental.pallas import tpu as pltpu
from jax.sharding import Mesh, PartitionSpec as P

D = 4096
HD = 128
HQ = 32
KVH = 4
STRETCH = 16
CAP = 1024
GROUP = 8
SLOTS = 4
ROWS = SLOTS * STRETCH
COLS = 80
SHARDS = 8
WIDE = COLS * SHARDS
HEADS = WIDE // HD
HALF = D // 2
ROPE_THETA = 1000000.0
LOG2E = 1.4426950408889634
AXES = ("tp", "z", "y", "xl", "xh")
VMEM_LIMIT = 48 * 1024 * 1024
NT = (((1,), (1,)), ((), ()))


def device_index(t, z, y, x):
    x = x % 4
    return ((((t % 2) * 4 + z % 4) * 4 + y % 4) * 2 + x % 2) * 2 + x // 2


def shift(array, dt=0, dz=0, dy=0, dx=0):
    pairs = [
        (device_index(t, z, y, x), device_index(t + dt, z + dz, y + dy, x + dx))
        for t in range(2)
        for z in range(4)
        for y in range(4)
        for x in range(4)
    ]
    return lax.ppermute(array, AXES, pairs)


def turn_kernel(w_ref, whole_ref, low_ref, high_ref):
    turned = w_ref[...].T
    whole_ref[...] = turned
    step = pl.program_id(0)
    half = pl.num_programs(0) // 2

    @pl.when(step < half)
    def _():
        low_ref[...] = turned

    @pl.when(step >= half)
    def _():
        high_ref[...] = turned


def turn(weight):
    steps = 8
    block = D // steps
    half = steps // 2
    return pl.pallas_call(
        turn_kernel,
        grid=(steps,),
        in_specs=[pl.BlockSpec((block, COLS), lambda i: (i, 0))],
        out_specs=[
            pl.BlockSpec((COLS, block), lambda i: (0, i)),
            pl.BlockSpec((COLS, block), lambda i: (0, jnp.minimum(i, half - 1))),
            pl.BlockSpec((COLS, block), lambda i: (0, jnp.maximum(i - half, 0))),
        ],
        out_shape=[
            jax.ShapeDtypeStruct((COLS, D), jnp.bfloat16),
            jax.ShapeDtypeStruct((COLS, HALF), jnp.bfloat16),
            jax.ShapeDtypeStruct((COLS, HALF), jnp.bfloat16),
        ],
        name="turn",
    )(weight)


def project_kernel(where, at_ref, bias_ref, *refs):
    count = len(where)
    pieces = refs[:count]
    rows = refs[count : count + 8]
    outs = refs[count + 8 : count + 16]
    weights, sem = refs[count + 16 :]
    copies = []
    for i, (piece, (dy, side, low, width)) in enumerate(zip(pieces, where)):
        start = pl.multiple_of(at_ref[dy * 2 + side] * COLS, 16)
        copies.append(
            pltpu.make_async_copy(
                piece,
                weights.at[pl.ds(start, COLS), pl.ds(low, width)],
                sem.at[i],
            )
        )
    for copy in copies:
        copy.start()
    for copy in copies:
        copy.wait()
    for row, out in zip(rows, outs):
        product = lax.dot_general(
            row[...], weights[...], NT, preferred_element_type=jnp.float32
        )
        out[...] = (product + bias_ref[...]).astype(jnp.bfloat16)


def project(places, bias, pieces, where, rows):
    return pl.pallas_call(
        functools.partial(project_kernel, where),
        in_specs=[
            pl.BlockSpec(memory_space=pltpu.SMEM),
            pl.BlockSpec(memory_space=pltpu.VMEM),
        ]
        + [pl.BlockSpec(memory_space=pl.ANY)] * len(pieces)
        + [pl.BlockSpec(memory_space=pltpu.VMEM)] * 8,
        out_specs=[pl.BlockSpec(memory_space=pltpu.VMEM)] * 8,
        out_shape=[jax.ShapeDtypeStruct((ROWS, WIDE), jnp.bfloat16)] * 8,
        scratch_shapes=[
            pltpu.VMEM((WIDE, D), jnp.bfloat16),
            pltpu.SemaphoreType.DMA((len(pieces),)),
        ],
        compiler_params=pltpu.CompilerParams(vmem_limit_bytes=VMEM_LIMIT),
        name="project",
    )(places, bias, *pieces, *rows)


def attend_kernel(group_ref, length_ref, cos_ref, sin_ref, *refs):
    blocks = refs[:8]
    cache_ref, out_ref, qkv = refs[8:]
    slot = pl.program_id(0)

    @pl.when(slot == 0)
    def _():
        for i, block in enumerate(blocks):
            qkv[group_ref[i]] = block[...]

    at = pl.ds(pl.multiple_of(slot * STRETCH, STRETCH), STRETCH)
    cosine = cos_ref[at, :]
    sine = sin_ref[at, :]
    length = length_ref[slot]

    def head(h):
        low = (h % HEADS) * HD
        return qkv[h // HEADS, at, low : low + HD]

    def rotated(h):
        u = head(h).astype(jnp.float32)
        return (u * cosine + pltpu.roll(u, HD // 2, 1) * sine).astype(jnp.bfloat16)

    scale = HD ** (-0.5) * LOG2E
    key_at = lax.broadcasted_iota(jnp.int32, (1, CAP), 1)
    hidden = jnp.where(key_at < length, 0.0, -jnp.inf)
    token = lax.broadcasted_iota(jnp.int32, (GROUP * STRETCH, STRETCH), 0) % STRETCH
    new_at = lax.broadcasted_iota(jnp.int32, (GROUP * STRETCH, STRETCH), 1)
    causal = new_at <= token
    for k in range(KVH):
        queries = jnp.concatenate(
            [rotated(k * GROUP + g) for g in range(GROUP)], axis=0
        )
        new_keys = rotated(HQ + k)
        new_values = head(HQ + KVH + k)
        keys = cache_ref[0, :, k * HD : (k + 1) * HD]
        values = cache_ref[0, :, (KVH + k) * HD : (KVH + k + 1) * HD]
        scores = (
            lax.dot_general(queries, keys, NT, preferred_element_type=jnp.float32)
            + hidden
        )
        new_scores = lax.dot_general(
            queries, new_keys, NT, preferred_element_type=jnp.float32
        )
        new_scores = jnp.where(causal, new_scores, -jnp.inf)
        top = jnp.maximum(
            jnp.max(scores, axis=1, keepdims=True),
            jnp.max(new_scores, axis=1, keepdims=True),
        )
        weights = jnp.exp2((scores - top) * scale)
        new_weights = jnp.exp2((new_scores - top) * scale)
        total = jnp.sum(weights, axis=1, keepdims=True) + jnp.sum(
            new_weights, axis=1, keepdims=True
        )
        mixed = jnp.dot(
            weights.astype(jnp.bfloat16), values, preferred_element_type=jnp.float32
        ) + jnp.dot(
            new_weights.astype(jnp.bfloat16),
            new_values,
            preferred_element_type=jnp.float32,
        )
        mixed = (mixed / total).astype(jnp.bfloat16)
        for g in range(GROUP):
            low = (k * GROUP + g) * HD
            out_ref[:, low : low + HD] = mixed[g * STRETCH : (g + 1) * STRETCH]


def attend(groups, lengths, cosine, sine, blocks, cache):
    whole = lambda shape: pl.BlockSpec(shape, lambda j: (0,) * len(shape))
    return pl.pallas_call(
        attend_kernel,
        grid=(SLOTS,),
        in_specs=[
            pl.BlockSpec(memory_space=pltpu.SMEM),
            pl.BlockSpec(memory_space=pltpu.SMEM),
            whole((ROWS, HD)),
            whole((ROWS, HD)),
        ]
        + [whole((ROWS, WIDE))] * 8
        + [pl.BlockSpec((1, CAP, 2 * KVH * HD), lambda j: (j, 0, 0))],
        out_specs=pl.BlockSpec((STRETCH, HQ * HD), lambda j: (j, 0)),
        out_shape=jax.ShapeDtypeStruct((ROWS, HQ * HD), jnp.bfloat16),
        scratch_shapes=[pltpu.VMEM((8, ROWS, WIDE), jnp.bfloat16)],
        compiler_params=pltpu.CompilerParams(vmem_limit_bytes=VMEM_LIMIT),
        name="attend",
    )(groups, lengths, cosine, sine, *blocks, cache)


def on_device(tokens, weight, bias, cache, lengths, slot_stream):
    t = lax.axis_index("tp")
    z = lax.axis_index("z")
    y = lax.axis_index("y")
    xl = lax.axis_index("xl")
    group = t * 4 + z
    index = (group * 4 + y) * 2 + xl

    along = {dz: shift(tokens, dz=dz) for dz in (1, 3, 2)}
    along[0] = tokens
    steps = [(dt, dz) for dt in range(2) for dz in range(4)]
    rows = [along[dz] if dt == 0 else shift(along[dz], dt=1) for dt, dz in steps]

    whole, low, high = turn(weight)
    one, three = shift(whole, dy=1), shift(whole, dy=3)
    two_low, two_high = shift(low, dy=2), shift(high, dy=2)
    pieces = [
        (whole, 0, 0, 0, D),
        (one, 1, 0, 0, D),
        (three, 3, 0, 0, D),
        (two_low, 2, 0, 0, HALF),
        (two_high, 2, 0, HALF, HALF),
        (shift(low, dx=1), 0, 1, 0, HALF),
        (shift(high, dx=3), 0, 1, HALF, HALF),
        (shift(one, dx=1), 1, 1, 0, D),
        (shift(three, dx=3), 3, 1, 0, D),
        (shift(two_low, dx=1), 2, 1, 0, HALF),
        (shift(two_high, dx=3), 2, 1, HALF, HALF),
    ]
    places = jnp.stack(
        [
            ((y - dy) % 4) * 2 + (xl if side == 0 else 1 - xl)
            for dy in range(4)
            for side in range(2)
        ]
    ).astype(jnp.int32)
    bias_cols = lax.dynamic_slice_in_dim(bias, group * WIDE, WIDE, 0)
    bias_cols = bias_cols.astype(jnp.float32)[None, :]

    my_slots = index * SLOTS + jnp.arange(SLOTS, dtype=jnp.int32)
    my_lengths = jnp.take(lengths, jnp.take(slot_stream, my_slots)).astype(jnp.int32)
    positions = (my_lengths[:, None] + jnp.arange(STRETCH, dtype=jnp.int32)).reshape(-1)
    frequency = ROPE_THETA ** (
        -(jnp.arange(HD // 2, dtype=jnp.float32) * 2.0) / HD
    )
    angles = positions.astype(jnp.float32)[:, None] * frequency[None, :]
    cosine, sine = jnp.cos(angles), jnp.sin(angles)
    cosine = jnp.concatenate([cosine, cosine], axis=1)
    sine = jnp.concatenate([-sine, sine], axis=1)

    parts = project(
        places, bias_cols, [p[0] for p in pieces], tuple(p[1:] for p in pieces), rows
    )
    home = [
        part if (dt, dz) == (0, 0) else shift(part, dt=-dt, dz=-dz)
        for part, (dt, dz) in zip(parts, steps)
    ]
    groups = jnp.stack(
        [((t + dt) % 2) * 4 + (z + dz) % 4 for dt, dz in steps]
    ).astype(jnp.int32)
    return attend(groups, my_lengths, cosine, sine, home, cache)


def solution(mesh):
    fine = Mesh(mesh.devices.reshape(2, 4, 4, 2, 2), AXES)
    part = ("xh", "tp", "z", "y", "xl")
    in_specs = (
        P(part, None),
        P(None, ("tp", "z", "y", "xl")),
        P(),
        P(part, None, None),
        P("xh"),
        P("xh"),
    )
    return jax.shard_map(
        on_device,
        mesh=fine,
        in_specs=in_specs,
        out_specs=P(part, None),
        check_vma=False,
    )
```

```python
import functools

import jax
import jax.numpy as jnp
from jax import lax
from jax.experimental import pallas as pl
from jax.experimental.pallas import tpu as pltpu
from jax.sharding import Mesh, PartitionSpec as P

D = 4096
HD = 128
HQ = 32
KVH = 4
STRETCH = 16
CAP = 1024
GROUP = 8
SLOTS = 4
ROWS = SLOTS * STRETCH
COLS = 80
SHARDS = 8
WIDE = COLS * SHARDS
HEADS = WIDE // HD
HALF = D // 2
ROPE_THETA = 1000000.0
LOG2E = 1.4426950408889634
AXES = ("tp", "z", "y", "xl", "xh")
NEAR = 4 * ROWS
PROJECT_VMEM = 56 * 1024 * 1024
ATTEND_VMEM = 56 * 1024 * 1024
NT = (((1,), (1,)), ((), ()))


def device_index(t, z, y, x):
    x = x % 4
    return ((((t % 2) * 4 + z % 4) * 4 + y % 4) * 2 + x % 2) * 2 + x // 2


def shift(array, dt=0, dz=0, dy=0, dx=0):
    pairs = [
        (device_index(t, z, y, x), device_index(t + dt, z + dz, y + dy, x + dx))
        for t in range(2)
        for z in range(4)
        for y in range(4)
        for x in range(4)
    ]
    return lax.ppermute(array, AXES, pairs)


def project_kernel(where, at_ref, bias_ref, *refs):
    count = len(where)
    pieces = refs[:count]
    rows = refs[count : count + 2]
    out = refs[count + 2]
    tokens, weights, sem = refs[count + 3 :]
    copies = [[], []]
    for i, row in enumerate(rows):
        for half in range(2):
            span = pl.ds(half * HALF, HALF)
            copies[half].append(
                pltpu.make_async_copy(
                    row.at[:, span],
                    tokens.at[pl.ds(i * NEAR, NEAR), span],
                    sem.at[half * 20 + i],
                )
            )
    for i, (piece, (dy, side, *halves)) in enumerate(zip(pieces, where)):
        start = pl.multiple_of(at_ref[dy * 2 + side] * COLS, 16)
        for half in halves:
            span = pl.ds((half - halves[0]) * HALF, HALF)
            copies[half].append(
                pltpu.make_async_copy(
                    piece.at[:, span],
                    weights.at[pl.ds(start, COLS), pl.ds(half * HALF, HALF)],
                    sem.at[half * 20 + 2 + i],
                )
            )
    for half in range(2):
        for copy in copies[half]:
            copy.start()
    total = bias_ref[...]
    for half in range(2):
        for copy in copies[half]:
            copy.wait()
        span = pl.ds(half * HALF, HALF)
        total = total + lax.dot_general(
            tokens[:, span], weights[:, span], NT, preferred_element_type=jnp.float32
        )
    total = total.astype(jnp.bfloat16)
    mine = at_ref[8]
    out[pl.ds(mine * 4, 4)] = total[:NEAR].reshape(4, ROWS, WIDE)
    out[pl.ds((1 - mine) * 4, 4)] = total[NEAR:].reshape(4, ROWS, WIDE)


def project(places, bias, pieces, where, rows):
    return pl.pallas_call(
        functools.partial(project_kernel, where),
        in_specs=[
            pl.BlockSpec(memory_space=pltpu.SMEM),
            pl.BlockSpec(memory_space=pltpu.VMEM),
        ]
        + [pl.BlockSpec(memory_space=pltpu.HBM)] * (len(pieces) + 2),
        out_specs=pl.BlockSpec(memory_space=pltpu.VMEM),
        out_shape=jax.ShapeDtypeStruct((8, ROWS, WIDE), jnp.bfloat16),
        scratch_shapes=[
            pltpu.VMEM((2 * NEAR, D), jnp.bfloat16),
            pltpu.VMEM((WIDE, D), jnp.bfloat16),
            pltpu.SemaphoreType.DMA((40,)),
        ],
        compiler_params=pltpu.CompilerParams(vmem_limit_bytes=PROJECT_VMEM),
        name="project",
    )(places, bias, *pieces, *rows)


def attend_kernel(length_ref, cos_ref, sin_ref, qkv, cache_ref, out_ref):
    slot = pl.program_id(0)
    at = pl.ds(pl.multiple_of(slot * STRETCH, STRETCH), STRETCH)
    cosine = cos_ref[at, :]
    sine = sin_ref[at, :]
    length = length_ref[slot]

    def head(h):
        low = (h % HEADS) * HD
        return qkv[h // HEADS, at, low : low + HD]

    def rotated(h):
        u = head(h).astype(jnp.float32)
        return (u * cosine + pltpu.roll(u, HD // 2, 1) * sine).astype(jnp.bfloat16)

    scale = HD ** (-0.5) * LOG2E
    key_at = lax.broadcasted_iota(jnp.int32, (1, CAP), 1)
    hidden = jnp.where(key_at < length, 0.0, -jnp.inf)
    token = lax.broadcasted_iota(jnp.int32, (GROUP * STRETCH, STRETCH), 0) % STRETCH
    new_at = lax.broadcasted_iota(jnp.int32, (GROUP * STRETCH, STRETCH), 1)
    causal = new_at <= token
    for k in range(KVH):
        queries = jnp.concatenate(
            [rotated(k * GROUP + g) for g in range(GROUP)], axis=0
        )
        new_keys = rotated(HQ + k)
        new_values = head(HQ + KVH + k)
        keys = cache_ref[0, :, k * HD : (k + 1) * HD]
        values = cache_ref[0, :, (KVH + k) * HD : (KVH + k + 1) * HD]
        scores = (
            lax.dot_general(queries, keys, NT, preferred_element_type=jnp.float32)
            + hidden
        )
        new_scores = lax.dot_general(
            queries, new_keys, NT, preferred_element_type=jnp.float32
        )
        new_scores = jnp.where(causal, new_scores, -jnp.inf)
        top = jnp.maximum(
            jnp.max(scores, axis=1, keepdims=True),
            jnp.max(new_scores, axis=1, keepdims=True),
        )
        weights = jnp.exp2((scores - top) * scale)
        new_weights = jnp.exp2((new_scores - top) * scale)
        total = jnp.sum(weights, axis=1, keepdims=True) + jnp.sum(
            new_weights, axis=1, keepdims=True
        )
        mixed = jnp.dot(
            weights.astype(jnp.bfloat16), values, preferred_element_type=jnp.float32
        ) + jnp.dot(
            new_weights.astype(jnp.bfloat16),
            new_values,
            preferred_element_type=jnp.float32,
        )
        mixed = (mixed / total).astype(jnp.bfloat16)
        for g in range(GROUP):
            low = (k * GROUP + g) * HD
            out_ref[:, low : low + HD] = mixed[g * STRETCH : (g + 1) * STRETCH]


def attend(lengths, cosine, sine, qkv, cache):
    whole = lambda shape: pl.BlockSpec(shape, lambda j: (0,) * len(shape))
    return pl.pallas_call(
        attend_kernel,
        grid=(SLOTS,),
        in_specs=[
            pl.BlockSpec(memory_space=pltpu.SMEM),
            whole((ROWS, HD)),
            whole((ROWS, HD)),
            whole((8, ROWS, WIDE)),
            pl.BlockSpec((1, CAP, 2 * KVH * HD), lambda j: (j, 0, 0)),
        ],
        out_specs=pl.BlockSpec((STRETCH, HQ * HD), lambda j: (j, 0)),
        out_shape=jax.ShapeDtypeStruct((ROWS, HQ * HD), jnp.bfloat16),
        compiler_params=pltpu.CompilerParams(vmem_limit_bytes=ATTEND_VMEM),
        name="attend",
    )(lengths, cosine, sine, qkv, cache)


def on_device(tokens, weight, bias, cache, lengths, slot_stream):
    t = lax.axis_index("tp")
    z = lax.axis_index("z")
    y = lax.axis_index("y")
    xl = lax.axis_index("xl")
    group = t * 4 + z
    index = (group * 4 + y) * 2 + xl

    copies = jnp.broadcast_to(tokens[None], (4, ROWS, D)).reshape(NEAR, D)
    mine = lax.all_to_all(copies, "z", split_axis=0, concat_axis=0, tiled=True)

    own = weight.T
    one, three, own_side = shift(own, dy=1), shift(own, dy=3), shift(own, dx=1)
    one, three, own_side, own = lax.optimization_barrier((one, three, own_side, own))
    two, one_side, three_side = shift(own, dy=2), shift(one, dx=3), shift(three, dx=1)
    two, one_side, three_side, mine = lax.optimization_barrier(
        (two, one_side, three_side, mine)
    )
    rows = [mine, shift(mine, dt=1)]
    two_low, two_high = shift(two[:, :HALF], dx=1), shift(two[:, HALF:], dx=3)
    pieces = [own, one, three, two, own_side, one_side, three_side, two_low, two_high]
    where = [
        (0, 0, 0, 1),
        (1, 0, 0, 1),
        (3, 0, 0, 1),
        (2, 0, 0, 1),
        (0, 1, 0, 1),
        (1, 1, 0, 1),
        (3, 1, 0, 1),
        (2, 1, 0),
        (2, 1, 1),
    ]

    places = jnp.stack(
        [
            ((y - dy) % 4) * 2 + (xl if side == 0 else 1 - xl)
            for dy in range(4)
            for side in range(2)
        ]
        + [t]
    ).astype(jnp.int32)
    bias_cols = lax.dynamic_slice_in_dim(bias, group * WIDE, WIDE, 0)
    bias_cols = bias_cols.astype(jnp.float32)[None, :]

    my_slots = index * SLOTS + jnp.arange(SLOTS, dtype=jnp.int32)
    my_lengths = jnp.take(lengths, jnp.take(slot_stream, my_slots)).astype(jnp.int32)
    positions = (my_lengths[:, None] + jnp.arange(STRETCH, dtype=jnp.int32)).reshape(-1)
    frequency = ROPE_THETA ** (
        -(jnp.arange(HD // 2, dtype=jnp.float32) * 2.0) / HD
    )
    angles = positions.astype(jnp.float32)[:, None] * frequency[None, :]
    cosine, sine = jnp.cos(angles), jnp.sin(angles)
    cosine = jnp.concatenate([cosine, cosine], axis=1)
    sine = jnp.concatenate([-sine, sine], axis=1)

    parts = project(places, bias_cols, pieces, tuple(where), rows)
    qkv = lax.all_to_all(parts, ("tp", "z"), split_axis=0, concat_axis=0, tiled=True)
    return attend(my_lengths, cosine, sine, qkv, cache)


def solution(mesh):
    fine = Mesh(mesh.devices.reshape(2, 4, 4, 2, 2), AXES)
    part = ("xh", "tp", "z", "y", "xl")
    in_specs = (
        P(part, None),
        P(None, ("tp", "z", "y", "xl")),
        P(),
        P(part, None, None),
        P("xh"),
        P("xh"),
    )
    return jax.shard_map(
        on_device,
        mesh=fine,
        in_specs=in_specs,
        out_specs=P(part, None),
        check_vma=False,
    )
```

```python
import functools

import jax
import jax.numpy as jnp
from jax import lax
from jax.experimental import pallas as pl
from jax.experimental.pallas import tpu as pltpu
from jax.sharding import Mesh, PartitionSpec as P

D = 4096
HD = 128
HQ = 32
KVH = 4
STRETCH = 16
CAP = 1024
GROUP = 8
SLOTS = 4
ROWS = SLOTS * STRETCH
COLS = 80
SHARDS = 8
WIDE = COLS * SHARDS
HEADS = WIDE // HD
HALF = D // 2
ROPE_THETA = 1000000.0
LOG2E = 1.4426950408889634
AXES = ("tp", "z", "y", "xl", "xh")
NEAR = 4 * ROWS
WINDOW = 256
PROJECT_VMEM = 56 * 1024 * 1024
ATTEND_VMEM = 56 * 1024 * 1024
NT = (((1,), (1,)), ((), ()))


def device_index(t, z, y, x):
    x = x % 4
    return ((((t % 2) * 4 + z % 4) * 4 + y % 4) * 2 + x % 2) * 2 + x // 2


def shift(array, dt=0, dz=0, dy=0, dx=0):
    pairs = [
        (device_index(t, z, y, x), device_index(t + dt, z + dz, y + dy, x + dx))
        for t in range(2)
        for z in range(4)
        for y in range(4)
        for x in range(4)
    ]
    return lax.ppermute(array, AXES, pairs)


def load(near, other, pieces, where, at_ref, tokens, weights, sem):
    copies = [[], []]
    count = 0
    for half in range(2):
        span = pl.ds(half * HALF, HALF)
        moves = [(near.at[:, span], tokens.at[pl.ds(0, NEAR), span])]
        moves.append((other.at[:, span], tokens.at[pl.ds(NEAR, NEAR), span]))
        for piece, (place, *halves) in zip(pieces, where):
            if half in halves:
                start = pl.multiple_of(at_ref[place], 16)
                source = piece.at[:, pl.ds((half - halves[0]) * HALF, HALF)]
                moves.append((source, weights.at[pl.ds(start, COLS), span]))
        for source, target in moves:
            copies[half].append(pltpu.make_async_copy(source, target, sem.at[count]))
            count += 1
    for half in range(2):
        for copy in copies[half]:
            copy.start()
    return copies


def multiply(copies, tokens, weights, total):
    for half in range(2):
        for copy in copies[half]:
            copy.wait()
        span = pl.ds(half * HALF, HALF)
        total = total + lax.dot_general(
            tokens[:, span], weights[:, span], NT, preferred_element_type=jnp.float32
        )
    return total


def project_first_kernel(where, at_ref, bias_ref, near, other, *refs):
    pieces = refs[:-4]
    out, tokens, weights, sem = refs[-4:]
    copies = load(near, other, pieces, where, at_ref, tokens, weights, sem)
    start = pl.multiple_of(at_ref[16], 16)
    weights[pl.ds(start, 2 * COLS), :] = jnp.zeros((2 * COLS, D), jnp.bfloat16)
    out[...] = multiply(copies, tokens, weights, bias_ref[...])


def project_last_kernel(where, at_ref, total_ref, near, other, *refs):
    pieces = refs[:-4]
    out, tokens, weights, sem = refs[-4:]
    copies = load(near, other, pieces, where, at_ref, tokens, weights, sem)
    shift_by = at_ref[17]
    for k in range(4):

        @pl.when(shift_by == 2 * k * STRETCH)
        def _():
            if k:
                weights[: 2 * k * STRETCH, :] = jnp.zeros(
                    (2 * k * STRETCH, D), jnp.bfloat16
                )
            rest = 2 * k * STRETCH + 2 * COLS
            if rest < WINDOW:
                weights[rest:, :] = jnp.zeros((WINDOW - rest, D), jnp.bfloat16)

    total = multiply(copies, tokens, weights, jnp.zeros((1, WINDOW), jnp.float32))
    for block in range(8):
        out[at_ref[8 + block]] = total_ref[pl.ds(block * ROWS, ROWS), :].astype(
            jnp.bfloat16
        )
    for k in range(4):

        @pl.when(shift_by == 2 * k * STRETCH)
        def _():
            window = slice(k * HD, k * HD + WINDOW)
            done = (total_ref[:, window] + total).astype(jnp.bfloat16)
            for block in range(8):
                out[at_ref[8 + block], :, window] = done[
                    block * ROWS : (block + 1) * ROWS
                ]


def project(kernel, width, out_shape, places, whole, near, other, pieces, where):
    return pl.pallas_call(
        functools.partial(kernel, where),
        in_specs=[
            pl.BlockSpec(memory_space=pltpu.SMEM),
            pl.BlockSpec(memory_space=pltpu.VMEM),
        ]
        + [pl.BlockSpec(memory_space=pltpu.HBM)] * (len(pieces) + 2),
        out_specs=pl.BlockSpec(memory_space=pltpu.VMEM),
        out_shape=out_shape,
        scratch_shapes=[
            pltpu.VMEM((2 * NEAR, D), jnp.bfloat16),
            pltpu.VMEM((width, D), jnp.bfloat16),
            pltpu.SemaphoreType.DMA((20,)),
        ],
        compiler_params=pltpu.CompilerParams(vmem_limit_bytes=PROJECT_VMEM),
        cost_estimate=pl.CostEstimate(
            flops=4 * NEAR * width * D,
            bytes_accessed=2 * D * (2 * NEAR + width),
            transcendentals=0,
        ),
        name=kernel.__name__.removesuffix("_kernel"),
    )(places, whole, near, other, *pieces)


def attend_kernel(length_ref, cos_ref, sin_ref, qkv, cache_ref, out_ref):
    slot = pl.program_id(0)
    at = pl.ds(pl.multiple_of(slot * STRETCH, STRETCH), STRETCH)
    cosine = cos_ref[at, :]
    sine = sin_ref[at, :]
    length = length_ref[slot]

    def head(h):
        low = (h % HEADS) * HD
        return qkv[h // HEADS, at, low : low + HD]

    def rotated(h):
        u = head(h).astype(jnp.float32)
        return (u * cosine + pltpu.roll(u, HD // 2, 1) * sine).astype(jnp.bfloat16)

    scale = HD ** (-0.5) * LOG2E
    key_at = lax.broadcasted_iota(jnp.int32, (1, CAP), 1)
    hidden = jnp.where(key_at < length, 0.0, -jnp.inf)
    token = lax.broadcasted_iota(jnp.int32, (GROUP * STRETCH, STRETCH), 0) % STRETCH
    new_at = lax.broadcasted_iota(jnp.int32, (GROUP * STRETCH, STRETCH), 1)
    causal = new_at <= token
    for k in range(KVH):
        queries = jnp.concatenate(
            [rotated(k * GROUP + g) for g in range(GROUP)], axis=0
        )
        new_keys = rotated(HQ + k)
        new_values = head(HQ + KVH + k)
        keys = cache_ref[0, :, k * HD : (k + 1) * HD]
        values = cache_ref[0, :, (KVH + k) * HD : (KVH + k + 1) * HD]
        scores = (
            lax.dot_general(queries, keys, NT, preferred_element_type=jnp.float32)
            + hidden
        )
        new_scores = lax.dot_general(
            queries, new_keys, NT, preferred_element_type=jnp.float32
        )
        new_scores = jnp.where(causal, new_scores, -jnp.inf)
        top = jnp.maximum(
            jnp.max(scores, axis=1, keepdims=True),
            jnp.max(new_scores, axis=1, keepdims=True),
        )
        weights = jnp.exp2((scores - top) * scale)
        new_weights = jnp.exp2((new_scores - top) * scale)
        total = jnp.sum(weights, axis=1, keepdims=True) + jnp.sum(
            new_weights, axis=1, keepdims=True
        )
        mixed = jnp.dot(
            weights.astype(jnp.bfloat16), values, preferred_element_type=jnp.float32
        ) + jnp.dot(
            new_weights.astype(jnp.bfloat16),
            new_values,
            preferred_element_type=jnp.float32,
        )
        mixed = (mixed / total).astype(jnp.bfloat16)
        for g in range(GROUP):
            low = (k * GROUP + g) * HD
            out_ref[:, low : low + HD] = mixed[g * STRETCH : (g + 1) * STRETCH]


def attend(lengths, cosine, sine, qkv, cache):
    whole = lambda shape: pl.BlockSpec(shape, lambda j: (0,) * len(shape))
    return pl.pallas_call(
        attend_kernel,
        grid=(SLOTS,),
        in_specs=[
            pl.BlockSpec(memory_space=pltpu.SMEM),
            whole((ROWS, HD)),
            whole((ROWS, HD)),
            whole((8, ROWS, WIDE)),
            pl.BlockSpec((1, CAP, 2 * KVH * HD), lambda j: (j, 0, 0)),
        ],
        out_specs=pl.BlockSpec((STRETCH, HQ * HD), lambda j: (j, 0)),
        out_shape=jax.ShapeDtypeStruct((ROWS, HQ * HD), jnp.bfloat16),
        compiler_params=pltpu.CompilerParams(vmem_limit_bytes=ATTEND_VMEM),
        name="attend",
    )(lengths, cosine, sine, qkv, cache)


def on_device(tokens, weight, bias, cache, lengths, slot_stream):
    t = lax.axis_index("tp")
    z = lax.axis_index("z")
    y = lax.axis_index("y")
    xl = lax.axis_index("xl")
    group = t * 4 + z
    index = (group * 4 + y) * 2 + xl

    far_y = (y + 2) % 4
    places = []
    for dy in range(4):
        base = far_y * 2 * STRETCH if dy == 2 else (y - dy) % 4 * 2 * COLS
        places += [base + xl * COLS, base + (1 - xl) * COLS]
    for core in (t, 1 - t):
        places += [core * 4 + (z - dz) % 4 for dz in (0, 1, 3, 2)]
    places += [far_y * 2 * COLS, far_y * 2 * STRETCH]
    places = jnp.stack(places).astype(jnp.int32)
    bias_cols = lax.dynamic_slice_in_dim(bias, group * WIDE, WIDE, 0)
    bias_cols = bias_cols.astype(jnp.float32)[None, :]

    my_slots = index * SLOTS + jnp.arange(SLOTS, dtype=jnp.int32)
    my_lengths = jnp.take(lengths, jnp.take(slot_stream, my_slots)).astype(jnp.int32)
    positions = (my_lengths[:, None] + jnp.arange(STRETCH, dtype=jnp.int32)).reshape(-1)
    frequency = ROPE_THETA ** (
        -(jnp.arange(HD // 2, dtype=jnp.float32) * 2.0) / HD
    )
    angles = positions.astype(jnp.float32)[:, None] * frequency[None, :]
    cosine, sine = jnp.cos(angles), jnp.sin(angles)
    cosine = jnp.concatenate([cosine, cosine], axis=1)
    sine = jnp.concatenate([-sine, sine], axis=1)

    own = weight.T
    one, three, own_side = shift(own, dy=1), shift(own, dy=3), shift(own, dx=1)
    up, down = shift(tokens, dz=1), shift(tokens, dz=3)
    one, three, own_side, up, down, tokens, small = lax.optimization_barrier(
        (one, three, own_side, up, down, tokens, (places, bias_cols, my_lengths, cosine, sine))
    )
    places, bias_cols, my_lengths, cosine, sine = small
    two_side = shift(own_side, dy=2)
    one_side, three_side = shift(one, dx=3), shift(three, dx=1)
    far = shift(tokens, dz=2)
    near = jnp.concatenate([tokens, up, down, far])
    low, high = one[:, :HALF], three[:, HALF:]
    near, one_side, three_side, two_side, low, high = lax.optimization_barrier(
        (near, one_side, three_side, two_side, low, high)
    )
    two_low, two_high = shift(low, dy=1), shift(high, dy=3)
    other = shift(near, dt=1)

    total = project(
        project_first_kernel,
        WIDE,
        jax.ShapeDtypeStruct((2 * NEAR, WIDE), jnp.float32),
        places,
        bias_cols,
        near,
        other,
        [own, own_side, one, one_side, three, three_side],
        tuple((place, 0, 1) for place in (0, 1, 2, 3, 6, 7)),
    )
    parts = project(
        project_last_kernel,
        WINDOW,
        jax.ShapeDtypeStruct((8, ROWS, WIDE), jnp.bfloat16),
        places,
        total,
        near,
        other,
        [two_low, two_high, two_side],
        ((4, 0), (4, 1), (5, 0, 1)),
    )
    qkv = lax.all_to_all(parts, ("tp", "z"), split_axis=0, concat_axis=0, tiled=True)
    return attend(my_lengths, cosine, sine, qkv, cache)


def solution(mesh):
    fine = Mesh(mesh.devices.reshape(2, 4, 4, 2, 2), AXES)
    part = ("xh", "tp", "z", "y", "xl")
    in_specs = (
        P(part, None),
        P(None, ("tp", "z", "y", "xl")),
        P(),
        P(part, None, None),
        P("xh"),
        P("xh"),
    )
    return jax.shard_map(
        on_device,
        mesh=fine,
        in_specs=in_specs,
        out_specs=P(part, None),
        check_vma=False,
    )
```

```python
import functools

import jax
import jax.numpy as jnp
from jax import lax
from jax.experimental import pallas as pl
from jax.experimental.pallas import tpu as pltpu
from jax.sharding import Mesh, PartitionSpec as P

D = 4096
HD = 128
HQ = 32
KVH = 4
STRETCH = 16
CAP = 1024
GROUP = 8
SLOTS = 4
ROWS = SLOTS * STRETCH
COLS = 80
SHARDS = 8
WIDE = COLS * SHARDS
HEADS = WIDE // HD
HALF = D // 2
ROPE_THETA = 1000000.0
LOG2E = 1.4426950408889634
AXES = ("tp", "z", "y", "xl", "xh")
NEAR = 4 * ROWS
WINDOW = 256
CHUNK = 256
PROJECT_VMEM = 20 * 1024 * 1024
ATTEND_VMEM = 16 * 1024 * 1024
NT = (((1,), (1,)), ((), ()))


def device_index(t, z, y, x):
    x = x % 4
    return ((((t % 2) * 4 + z % 4) * 4 + y % 4) * 2 + x % 2) * 2 + x // 2


def shift(array, dt=0, dz=0, dy=0, dx=0):
    pairs = [
        (device_index(t, z, y, x), device_index(t + dt, z + dz, y + dy, x + dx))
        for t in range(2)
        for z in range(4)
        for y in range(4)
        for x in range(4)
    ]
    return lax.ppermute(array, AXES, pairs)


def gather(pieces, where, at_ref, weights):
    for piece, (place, low) in zip(pieces, where):
        start = pl.multiple_of(at_ref[place], 16)
        weights[pl.ds(start, COLS), low : low + piece.shape[1]] = piece[...]


def multiply(near, other, weights):
    return [
        lax.dot_general(rows[...], weights[...], NT, preferred_element_type=jnp.float32)
        for rows in (near, other)
    ]


def project_first_kernel(where, at_ref, bias_ref, near, other, *refs):
    pieces = refs[:-2]
    out, weights = refs[-2:]
    start = pl.multiple_of(at_ref[16], 16)
    weights[pl.ds(start, 2 * COLS), :] = jnp.zeros((2 * COLS, D), jnp.bfloat16)
    gather(pieces, where, at_ref, weights)
    first, second = multiply(near, other, weights)
    out[:NEAR] = first + bias_ref[...]
    out[NEAR:] = second + bias_ref[...]


def project_last_kernel(where, at_ref, total_ref, near, other, *refs):
    pieces = refs[:-2]
    out, weights = refs[-2:]
    shift_by = at_ref[17]
    for k in range(4):

        @pl.when(shift_by == 2 * k * STRETCH)
        def _():
            low, high = 2 * k * STRETCH, 2 * k * STRETCH + 2 * COLS
            if low:
                weights[:low, :] = jnp.zeros((low, D), jnp.bfloat16)
            if high < WINDOW:
                weights[high:, :] = jnp.zeros((WINDOW - high, D), jnp.bfloat16)

    gather(pieces, where, at_ref, weights)
    total = multiply(near, other, weights)
    for k in range(4):

        @pl.when(shift_by == 2 * k * STRETCH)
        def _():
            low, high = k * HD, k * HD + WINDOW
            for block in range(8):
                rows = slice(block * ROWS, (block + 1) * ROWS)
                here = slice(block % 4 * ROWS, (block % 4 + 1) * ROWS)
                done = total_ref[rows, low:high] + total[block // 4][here]
                home = at_ref[8 + block]
                out[home, :, low:high] = done.astype(jnp.bfloat16)
                if low:
                    out[home, :, :low] = total_ref[rows, :low].astype(jnp.bfloat16)
                if high < WIDE:
                    out[home, :, high:] = total_ref[rows, high:].astype(jnp.bfloat16)


def project(kernel, width, out_shape, places, whole, near, other, pieces, where):
    return pl.pallas_call(
        functools.partial(kernel, where),
        in_specs=[pl.BlockSpec(memory_space=pltpu.SMEM)]
        + [pl.BlockSpec(memory_space=pltpu.VMEM)] * (len(pieces) + 3),
        out_specs=pl.BlockSpec(memory_space=pltpu.VMEM),
        out_shape=out_shape,
        scratch_shapes=[pltpu.VMEM((width, D), jnp.bfloat16)],
        compiler_params=pltpu.CompilerParams(vmem_limit_bytes=PROJECT_VMEM),
        cost_estimate=pl.CostEstimate(
            flops=4 * NEAR * width * D,
            bytes_accessed=2 * D * (2 * NEAR + width),
            transcendentals=0,
        ),
        name=kernel.__name__.removesuffix("_kernel"),
    )(places, whole, near, other, *pieces)


def attend_kernel(length_ref, cos_ref, sin_ref, qkv, cache, out_ref, scores):
    scale = HD ** (-0.5) * LOG2E
    key_at = lax.broadcasted_iota(jnp.int32, (1, CAP), 1)
    token = lax.broadcasted_iota(jnp.int32, (GROUP * STRETCH, STRETCH), 0) % STRETCH
    causal = lax.broadcasted_iota(jnp.int32, (GROUP * STRETCH, STRETCH), 1) <= token

    def head(slot, h):
        low = (h % HEADS) * HD
        rows = slice(slot * STRETCH, (slot + 1) * STRETCH)
        return qkv[h // HEADS, rows, low : low + HD]

    def rotated(slot, h):
        rows = slice(slot * STRETCH, (slot + 1) * STRETCH)
        u = head(slot, h).astype(jnp.float32)
        turned = pltpu.roll(u, HD // 2, 1) * sin_ref[rows, :]
        return (u * cos_ref[rows, :] + turned).astype(jnp.bfloat16)

    def score(slot, k):
        hidden = jnp.where(key_at < length_ref[slot], 0.0, -jnp.inf)
        queries = [rotated(slot, k * GROUP + g) for g in range(GROUP)]
        queries = jnp.concatenate(queries, axis=0)
        new = lax.dot_general(
            queries, rotated(slot, HQ + k), NT, preferred_element_type=jnp.float32
        )
        new = jnp.where(causal, new, -jnp.inf)
        highest = None
        for low in range(0, CAP, CHUNK):
            keys = cache[slot, low : low + CHUNK, k * HD : (k + 1) * HD]
            part = lax.dot_general(
                queries, keys, NT, preferred_element_type=jnp.float32
            )
            part = part + hidden[:, low : low + CHUNK]
            scores[k % 2, :, low : low + CHUNK] = part
            part = jnp.maximum(part[:, :HD], part[:, HD:])
            highest = part if highest is None else jnp.maximum(highest, part)
        top = jnp.maximum(
            jnp.max(highest, axis=1, keepdims=True), jnp.max(new, axis=1, keepdims=True)
        )
        return top * scale, new

    def mix(slot, k, base, new):
        new = jnp.exp2(new * scale - base)
        mixed = jnp.dot(
            new.astype(jnp.bfloat16),
            head(slot, HQ + KVH + k),
            preferred_element_type=jnp.float32,
        )
        total = None
        for low in range(0, CAP, CHUNK):
            part = jnp.exp2(scores[k % 2, :, low : low + CHUNK] * scale - base)
            values = cache[slot, low : low + CHUNK, (KVH + k) * HD : (KVH + k + 1) * HD]
            mixed = mixed + jnp.dot(
                part.astype(jnp.bfloat16), values, preferred_element_type=jnp.float32
            )
            part = part[:, :HD] + part[:, HD:]
            total = part if total is None else total + part
        total = jnp.sum(total, axis=1, keepdims=True) + jnp.sum(
            new, axis=1, keepdims=True
        )
        mixed = (mixed / total).astype(jnp.bfloat16)
        for g in range(GROUP):
            low = (k * GROUP + g) * HD
            out_ref[slot * STRETCH : (slot + 1) * STRETCH, low : low + HD] = mixed[
                g * STRETCH : (g + 1) * STRETCH
            ]

    pairs = [(slot, k) for slot in range(SLOTS) for k in range(KVH)]
    ahead = None
    for pair in pairs:
        state = score(*pair)
        if ahead is not None:
            mix(*ahead)
        ahead = (*pair, *state)
    mix(*ahead)


def attend(lengths, cosine, sine, qkv, cache):
    return pl.pallas_call(
        attend_kernel,
        in_specs=[pl.BlockSpec(memory_space=pltpu.SMEM)]
        + [pl.BlockSpec(memory_space=pltpu.VMEM)] * 4,
        out_specs=pl.BlockSpec(memory_space=pltpu.VMEM),
        out_shape=jax.ShapeDtypeStruct((ROWS, HQ * HD), jnp.bfloat16),
        scratch_shapes=[pltpu.VMEM((2, GROUP * STRETCH, CAP), jnp.float32)],
        compiler_params=pltpu.CompilerParams(vmem_limit_bytes=ATTEND_VMEM),
        name="attend",
    )(lengths, cosine, sine, qkv, cache)


def on_device(tokens, weight, bias, cache, lengths, slot_stream):
    t = lax.axis_index("tp")
    z = lax.axis_index("z")
    y = lax.axis_index("y")
    xl = lax.axis_index("xl")
    group = t * 4 + z
    index = (group * 4 + y) * 2 + xl

    far_y = (y + 2) % 4
    places = []
    for dy in range(4):
        base = far_y * 2 * STRETCH if dy == 2 else (y - dy) % 4 * 2 * COLS
        places += [base + xl * COLS, base + (1 - xl) * COLS]
    for core in (t, 1 - t):
        places += [core * 4 + (z - dz) % 4 for dz in (0, 1, 3, 2)]
    places += [far_y * 2 * COLS, far_y * 2 * STRETCH]
    places = jnp.stack(places).astype(jnp.int32)
    bias_cols = lax.dynamic_slice_in_dim(bias, group * WIDE, WIDE, 0)
    bias_cols = bias_cols.astype(jnp.float32)[None, :]

    my_slots = index * SLOTS + jnp.arange(SLOTS, dtype=jnp.int32)
    my_lengths = jnp.take(lengths, jnp.take(slot_stream, my_slots)).astype(jnp.int32)
    positions = (my_lengths[:, None] + jnp.arange(STRETCH, dtype=jnp.int32)).reshape(-1)
    frequency = ROPE_THETA ** (
        -(jnp.arange(HD // 2, dtype=jnp.float32) * 2.0) / HD
    )
    angles = positions.astype(jnp.float32)[:, None] * frequency[None, :]
    cosine, sine = jnp.cos(angles), jnp.sin(angles)
    cosine = jnp.concatenate([cosine, cosine], axis=1)
    sine = jnp.concatenate([-sine, sine], axis=1)

    own = weight.T
    one, three, own_side = shift(own, dy=1), shift(own, dy=3), shift(own, dx=1)
    up, down = shift(tokens, dz=1), shift(tokens, dz=3)
    one, three, own_side, up, down, tokens, small = lax.optimization_barrier(
        (one, three, own_side, up, down, tokens, (places, bias_cols, my_lengths, cosine, sine))
    )
    places, bias_cols, my_lengths, cosine, sine = small
    two_side = shift(own_side, dy=2)
    one_side, three_side = shift(one, dx=3), shift(three, dx=1)
    far = shift(tokens, dz=2)
    near = jnp.concatenate([tokens, up, down, far])
    low, high = one[:, :HALF], three[:, HALF:]
    near, one_side, three_side, two_side, low, high = lax.optimization_barrier(
        (near, one_side, three_side, two_side, low, high)
    )
    two_low, two_high = shift(low, dy=1), shift(high, dy=3)
    other = shift(near, dt=1)

    total = project(
        project_first_kernel,
        WIDE,
        jax.ShapeDtypeStruct((2 * NEAR, WIDE), jnp.float32),
        places,
        bias_cols,
        near,
        other,
        [own, own_side, one, one_side, three, three_side],
        tuple((place, 0) for place in (0, 1, 2, 3, 6, 7)),
    )
    parts = project(
        project_last_kernel,
        WINDOW,
        jax.ShapeDtypeStruct((8, ROWS, WIDE), jnp.bfloat16),
        places,
        total,
        near,
        other,
        [two_low, two_high, two_side],
        ((4, 0), (4, HALF), (5, 0)),
    )
    qkv = lax.all_to_all(parts, ("tp", "z"), split_axis=0, concat_axis=0, tiled=True)
    return attend(my_lengths, cosine, sine, qkv, cache)


def solution(mesh):
    fine = Mesh(mesh.devices.reshape(2, 4, 4, 2, 2), AXES)
    part = ("xh", "tp", "z", "y", "xl")
    in_specs = (
        P(part, None),
        P(None, ("tp", "z", "y", "xl")),
        P(),
        P(part, None, None),
        P("xh"),
        P("xh"),
    )
    return jax.shard_map(
        on_device,
        mesh=fine,
        in_specs=in_specs,
        out_specs=P(part, None),
        check_vma=False,
    )
```

```python
import functools

import jax
import jax.numpy as jnp
from jax import lax
from jax.experimental import pallas as pl
from jax.experimental.pallas import tpu as pltpu
from jax.sharding import Mesh, PartitionSpec as P

D = 4096
HD = 128
HQ = 32
KVH = 4
STRETCH = 16
CAP = 1024
GROUP = 8
SLOTS = 4
ROWS = SLOTS * STRETCH
COLS = 80
SHARDS = 8
WIDE = COLS * SHARDS
HEADS = WIDE // HD
HALF = D // 2
ROPE_THETA = 1000000.0
LOG2E = 1.4426950408889634
AXES = ("tp", "z", "y", "xl", "xh")
NEAR = 4 * ROWS
WINDOW = 256
CHUNK = 256
PROJECT_VMEM = 14 * 1024 * 1024
ATTEND_VMEM = 8 * 1024 * 1024
NT = (((1,), (1,)), ((), ()))
HOME = [(0, 2), (1, 2), (0, 1), (1, 1), (0, 3), (1, 3), (1, 0), (0, 0)]


def device_index(t, z, y, x):
    x = x % 4
    return ((((t % 2) * 4 + z % 4) * 4 + y % 4) * 2 + x % 2) * 2 + x // 2


def shift(array, dt=0, dz=0, dy=0, dx=0):
    pairs = [
        (device_index(t, z, y, x), device_index(t + dt, z + dz, y + dy, x + dx))
        for t in range(2)
        for z in range(4)
        for y in range(4)
        for x in range(4)
    ]
    return lax.ppermute(array, AXES, pairs)


def copy_rows_kernel(rows, early, out, sem):
    copy = pltpu.make_async_copy(rows, out, sem)
    copy.start()
    copy.wait()


def copy_rows(rows, early):
    return pl.pallas_call(
        copy_rows_kernel,
        in_specs=[pl.BlockSpec(memory_space=pltpu.HBM), pl.BlockSpec(memory_space=pl.ANY)],
        out_specs=pl.BlockSpec(memory_space=pltpu.VMEM),
        out_shape=jax.ShapeDtypeStruct((ROWS, D), jnp.bfloat16),
        scratch_shapes=[pltpu.SemaphoreType.DMA],
        compiler_params=pltpu.CompilerParams(vmem_limit_bytes=8 * 1024 * 1024),
        name="copy_rows",
    )(rows, early)


def gather(pieces, where, at_ref, weights):
    for piece, (place, low) in zip(pieces, where):
        start = pl.multiple_of(at_ref[place], 16)
        weights[pl.ds(start, COLS), low : low + piece.shape[1]] = piece[...]


def multiply(rows, weights):
    return [
        lax.dot_general(
            rows[low : low + NEAR, :],
            weights[...],
            NT,
            preferred_element_type=jnp.float32,
        )
        for low in (0, NEAR)
    ]


def project_first_kernel(where, at_ref, bias_ref, *refs):
    pieces, blocks = refs[:-7], refs[-7:-3]
    out, rows, weights = refs[-3:]
    start = pl.multiple_of(at_ref[8], 16)
    weights[pl.ds(start, 2 * COLS), :] = jnp.zeros((2 * COLS, D), jnp.bfloat16)
    gather(pieces, where, at_ref, weights)
    low = 0
    for block in blocks:
        rows[low : low + block.shape[0], :] = block[...]
        low += block.shape[0]
    first, second = multiply(rows, weights)
    out[:NEAR] = first + bias_ref[...]
    out[NEAR:] = second + bias_ref[...]


def project_last_kernel(where, at_ref, total_ref, *refs):
    pieces, rows = refs[:-10], refs[-10]
    outs, weights = refs[-9:-1], refs[-1]
    shift_by = at_ref[9]
    for k in range(4):

        @pl.when(shift_by == 2 * k * STRETCH)
        def _():
            low, high = 2 * k * STRETCH, 2 * k * STRETCH + 2 * COLS
            if low:
                weights[:low, :] = jnp.zeros((low, D), jnp.bfloat16)
            if high < WINDOW:
                weights[high:, :] = jnp.zeros((WINDOW - high, D), jnp.bfloat16)

    gather(pieces, where, at_ref, weights)
    total = multiply(rows, weights)
    for k in range(4):

        @pl.when(shift_by == 2 * k * STRETCH)
        def _():
            low, high = k * HD, k * HD + WINDOW
            for block in range(8):
                span = slice(block * ROWS, (block + 1) * ROWS)
                here = slice(block % 4 * ROWS, (block % 4 + 1) * ROWS)
                done = total_ref[span, low:high] + total[block // 4][here]
                out = outs[HOME.index((block // 4, (0, 1, 3, 2)[block % 4]))]
                out[:, low:high] = done.astype(jnp.bfloat16)
                if low:
                    out[:, :low] = total_ref[span, :low].astype(jnp.bfloat16)
                if high < WIDE:
                    out[:, high:] = total_ref[span, high:].astype(jnp.bfloat16)


def project(kernel, width, out_shape, places, whole, operands, where):
    vmem = pl.BlockSpec(memory_space=pltpu.VMEM)
    return pl.pallas_call(
        functools.partial(kernel, where),
        in_specs=[pl.BlockSpec(memory_space=pltpu.SMEM)] + [vmem] * (len(operands) + 1),
        out_specs=jax.tree.map(lambda _: vmem, out_shape),
        out_shape=out_shape,
        scratch_shapes=[pltpu.VMEM((width, D), jnp.bfloat16)],
        compiler_params=pltpu.CompilerParams(vmem_limit_bytes=PROJECT_VMEM),
        cost_estimate=pl.CostEstimate(
            flops=4 * NEAR * width * D,
            bytes_accessed=2 * D * (2 * NEAR + width),
            transcendentals=0,
        ),
        name=kernel.__name__.removesuffix("_kernel"),
    )(places, whole, *operands)


def attend_kernel(group_ref, length_ref, cos_ref, sin_ref, cache, *refs):
    blocks, out_ref, qkv, scores = refs[:8], *refs[8:]
    for i, block in enumerate(blocks):
        qkv[group_ref[i]] = block[...]
    scale = HD ** (-0.5) * LOG2E
    key_at = lax.broadcasted_iota(jnp.int32, (1, CAP), 1)
    token = lax.broadcasted_iota(jnp.int32, (GROUP * STRETCH, STRETCH), 0) % STRETCH
    causal = lax.broadcasted_iota(jnp.int32, (GROUP * STRETCH, STRETCH), 1) <= token

    def head(slot, h):
        low = (h % HEADS) * HD
        rows = slice(slot * STRETCH, (slot + 1) * STRETCH)
        return qkv[h // HEADS, rows, low : low + HD]

    def rotated(slot, h):
        rows = slice(slot * STRETCH, (slot + 1) * STRETCH)
        u = head(slot, h).astype(jnp.float32)
        turned = pltpu.roll(u, HD // 2, 1) * sin_ref[rows, :]
        return (u * cos_ref[rows, :] + turned).astype(jnp.bfloat16)

    def score(slot, k):
        hidden = jnp.where(key_at < length_ref[slot], 0.0, -jnp.inf)
        queries = [rotated(slot, k * GROUP + g) for g in range(GROUP)]
        queries = jnp.concatenate(queries, axis=0)
        new = lax.dot_general(
            queries, rotated(slot, HQ + k), NT, preferred_element_type=jnp.float32
        )
        new = jnp.where(causal, new, -jnp.inf)
        highest = None
        for low in range(0, CAP, CHUNK):
            keys = cache[slot, low : low + CHUNK, k * HD : (k + 1) * HD]
            part = lax.dot_general(
                queries, keys, NT, preferred_element_type=jnp.float32
            )
            part = part + hidden[:, low : low + CHUNK]
            scores[k % 2, :, low : low + CHUNK] = part
            part = jnp.maximum(part[:, :HD], part[:, HD:])
            highest = part if highest is None else jnp.maximum(highest, part)
        top = jnp.maximum(
            jnp.max(highest, axis=1, keepdims=True), jnp.max(new, axis=1, keepdims=True)
        )
        return top * scale, new

    def mix(slot, k, base, new):
        new = jnp.exp2(new * scale - base)
        mixed = jnp.dot(
            new.astype(jnp.bfloat16),
            head(slot, HQ + KVH + k),
            preferred_element_type=jnp.float32,
        )
        total = None
        for low in range(0, CAP, CHUNK):
            part = jnp.exp2(scores[k % 2, :, low : low + CHUNK] * scale - base)
            values = cache[slot, low : low + CHUNK, (KVH + k) * HD : (KVH + k + 1) * HD]
            mixed = mixed + jnp.dot(
                part.astype(jnp.bfloat16), values, preferred_element_type=jnp.float32
            )
            part = part[:, :HD] + part[:, HD:]
            total = part if total is None else total + part
        total = jnp.sum(total, axis=1, keepdims=True) + jnp.sum(
            new, axis=1, keepdims=True
        )
        mixed = (mixed / total).astype(jnp.bfloat16)
        for g in range(GROUP):
            low = (k * GROUP + g) * HD
            out_ref[slot * STRETCH : (slot + 1) * STRETCH, low : low + HD] = mixed[
                g * STRETCH : (g + 1) * STRETCH
            ]

    pairs = [(slot, k) for slot in range(SLOTS) for k in range(KVH)]
    ahead = None
    for pair in pairs:
        state = score(*pair)
        if ahead is not None:
            mix(*ahead)
        ahead = (*pair, *state)
    mix(*ahead)


def attend(groups, lengths, cosine, sine, cache, blocks):
    return pl.pallas_call(
        attend_kernel,
        in_specs=[pl.BlockSpec(memory_space=pltpu.SMEM)] * 2
        + [pl.BlockSpec(memory_space=pltpu.VMEM)] * 11,
        out_specs=pl.BlockSpec(memory_space=pltpu.VMEM),
        out_shape=jax.ShapeDtypeStruct((ROWS, HQ * HD), jnp.bfloat16),
        scratch_shapes=[
            pltpu.VMEM((8, ROWS, WIDE), jnp.bfloat16),
            pltpu.VMEM((2, GROUP * STRETCH, CAP), jnp.float32),
        ],
        compiler_params=pltpu.CompilerParams(vmem_limit_bytes=ATTEND_VMEM),
        name="attend",
    )(groups, lengths, cosine, sine, cache, *blocks)


def on_device(tokens, weight, bias, cache, lengths, slot_stream):
    t = lax.axis_index("tp")
    z = lax.axis_index("z")
    y = lax.axis_index("y")
    xl = lax.axis_index("xl")
    group = t * 4 + z
    index = (group * 4 + y) * 2 + xl

    own = weight.T
    own_side, three, one = shift(own, dx=1), shift(own, dy=3), shift(own, dy=1)
    early = shift(jnp.zeros((16, HD), jnp.bfloat16), dt=1)
    late = copy_rows(tokens, early)
    late, bias, lengths, slot_stream = lax.optimization_barrier(
        (late, bias, lengths, slot_stream)
    )

    far_y = (y + 2) % 4
    places = []
    for dy in range(4):
        base = far_y * 2 * STRETCH if dy == 2 else (y - dy) % 4 * 2 * COLS
        places += [base + xl * COLS, base + (1 - xl) * COLS]
    places += [far_y * 2 * COLS, far_y * 2 * STRETCH]
    places = jnp.stack(places).astype(jnp.int32)
    groups = [(t + dt) % 2 * 4 + (z + dz) % 4 for dt, dz in HOME]
    groups = jnp.stack(groups).astype(jnp.int32)
    bias_cols = lax.dynamic_slice_in_dim(bias, group * WIDE, WIDE, 0)
    bias_cols = bias_cols.astype(jnp.float32)[None, :]

    my_slots = index * SLOTS + jnp.arange(SLOTS, dtype=jnp.int32)
    my_lengths = jnp.take(lengths, jnp.take(slot_stream, my_slots)).astype(jnp.int32)
    positions = (my_lengths[:, None] + jnp.arange(STRETCH, dtype=jnp.int32)).reshape(-1)
    frequency = ROPE_THETA ** (
        -(jnp.arange(HD // 2, dtype=jnp.float32) * 2.0) / HD
    )
    angles = positions.astype(jnp.float32)[:, None] * frequency[None, :]
    cosine, sine = jnp.cos(angles), jnp.sin(angles)
    cosine = jnp.concatenate([cosine, cosine], axis=1)
    sine = jnp.concatenate([-sine, sine], axis=1)

    up, down = shift(late, dz=1), shift(late, dz=3)
    own_side, three, one, tokens, late, small = lax.optimization_barrier(
        (own_side, three, one, tokens, late, (places, groups, bias_cols, my_lengths, cosine, sine))
    )
    places, groups, bias_cols, my_lengths, cosine, sine = small
    far = shift(late, dz=2)
    one_side, three_side = shift(one, dx=3), shift(three, dx=1)
    two_side = shift(own_side, dy=2)
    near = jnp.concatenate([tokens, up, down])
    low, high = one[:, :HALF], three[:, HALF:]
    two_side, one_side, three_side, far, near, low, high = lax.optimization_barrier(
        (two_side, one_side, three_side, far, near, low, high)
    )
    two_low, two_high = shift(low, dy=1), shift(high, dy=3)
    other = shift(near, dt=1)
    other_far = shift(far, dt=1)

    total, rows = project(
        project_first_kernel,
        WIDE,
        [
            jax.ShapeDtypeStruct((2 * NEAR, WIDE), jnp.float32),
            jax.ShapeDtypeStruct((2 * NEAR, D), jnp.bfloat16),
        ],
        places,
        bias_cols,
        [own, own_side, one, one_side, three, three_side, near, far, other, other_far],
        tuple((place, 0) for place in (0, 1, 2, 3, 6, 7)),
    )
    parts = project(
        project_last_kernel,
        WINDOW,
        [jax.ShapeDtypeStruct((ROWS, WIDE), jnp.bfloat16)] * 8,
        places,
        total,
        [two_low, two_high, two_side, rows],
        ((4, 0), (4, HALF), (5, 0)),
    )
    blocks = [
        shift(part, dt=-dt, dz=-dz) if dt or dz else part
        for part, (dt, dz) in zip(parts, HOME)
    ]
    return attend(groups, my_lengths, cosine, sine, cache, blocks)


def solution(mesh):
    fine = Mesh(mesh.devices.reshape(2, 4, 4, 2, 2), AXES)
    part = ("xh", "tp", "z", "y", "xl")
    in_specs = (
        P(part, None),
        P(None, ("tp", "z", "y", "xl")),
        P(),
        P(part, None, None),
        P("xh"),
        P("xh"),
    )
    return jax.shard_map(
        on_device,
        mesh=fine,
        in_specs=in_specs,
        out_specs=P(part, None),
        check_vma=False,
    )
```

```python
import functools

import jax
import jax.numpy as jnp
from jax import lax
from jax.experimental import pallas as pl
from jax.experimental.pallas import tpu as pltpu
from jax.sharding import Mesh, PartitionSpec as P

D = 4096
HD = 128
HQ = 32
KVH = 4
STRETCH = 16
CAP = 1024
GROUP = 8
SLOTS = 4
ROWS = SLOTS * STRETCH
COLS = 80
SHARDS = 8
WIDE = COLS * SHARDS
HEADS = WIDE // HD
HALF = D // 2
ROPE_THETA = 1000000.0
LOG2E = 1.4426950408889634
AXES = ("tp", "z", "y", "xl", "xh")
NEAR = 4 * ROWS
WINDOW = 256
CHUNK = 256
PROJECT_VMEM = 14 * 1024 * 1024
ATTEND_VMEM = 8 * 1024 * 1024
NT = (((1,), (1,)), ((), ()))
HOME = [(0, 2), (1, 2), (0, 1), (1, 1), (0, 3), (1, 3), (1, 0), (0, 0)]


def device_index(t, z, y, x):
    x = x % 4
    return ((((t % 2) * 4 + z % 4) * 4 + y % 4) * 2 + x % 2) * 2 + x // 2


def shift(array, dt=0, dz=0, dy=0, dx=0):
    pairs = [
        (device_index(t, z, y, x), device_index(t + dt, z + dz, y + dy, x + dx))
        for t in range(2)
        for z in range(4)
        for y in range(4)
        for x in range(4)
    ]
    return lax.ppermute(array, AXES, pairs)


def copy_rows_kernel(rows, early, out, sem):
    copy = pltpu.make_async_copy(rows, out, sem)
    copy.start()
    copy.wait()


def copy_rows(rows, early):
    return pl.pallas_call(
        copy_rows_kernel,
        in_specs=[pl.BlockSpec(memory_space=pltpu.HBM), pl.BlockSpec(memory_space=pl.ANY)],
        out_specs=pl.BlockSpec(memory_space=pltpu.VMEM),
        out_shape=jax.ShapeDtypeStruct((ROWS, D), jnp.bfloat16),
        scratch_shapes=[pltpu.SemaphoreType.DMA],
        compiler_params=pltpu.CompilerParams(vmem_limit_bytes=8 * 1024 * 1024),
        name="copy_rows",
    )(rows, early)


def gather(pieces, where, at_ref, weights):
    for piece, (place, low) in zip(pieces, where):
        start = pl.multiple_of(at_ref[place], 16)
        weights[pl.ds(start, COLS), low : low + piece.shape[1]] = piece[...]


def multiply(rows, weights):
    return [
        lax.dot_general(
            rows[low : low + NEAR, :],
            weights[...],
            NT,
            preferred_element_type=jnp.float32,
        )
        for low in (0, NEAR)
    ]


def project_first_kernel(where, at_ref, bias_ref, *refs):
    pieces, blocks = refs[:-7], refs[-7:-3]
    out, rows, weights = refs[-3:]
    start = pl.multiple_of(at_ref[8], 16)
    weights[pl.ds(start, 2 * COLS), :] = jnp.zeros((2 * COLS, D), jnp.bfloat16)
    gather(pieces, where, at_ref, weights)
    low = 0
    for block in blocks:
        rows[low : low + block.shape[0], :] = block[...]
        low += block.shape[0]
    first, second = multiply(rows, weights)
    out[:NEAR] = first + bias_ref[...]
    out[NEAR:] = second + bias_ref[...]


def project_last_kernel(where, at_ref, total_ref, *refs):
    pieces, rows = refs[:-10], refs[-10]
    outs, weights = refs[-9:-1], refs[-1]
    shift_by = at_ref[9]
    for k in range(4):

        @pl.when(shift_by == 2 * k * STRETCH)
        def _():
            low, high = 2 * k * STRETCH, 2 * k * STRETCH + 2 * COLS
            if low:
                weights[:low, :] = jnp.zeros((low, D), jnp.bfloat16)
            if high < WINDOW:
                weights[high:, :] = jnp.zeros((WINDOW - high, D), jnp.bfloat16)

    gather(pieces, where, at_ref, weights)
    total = multiply(rows, weights)
    for k in range(4):

        @pl.when(shift_by == 2 * k * STRETCH)
        def _():
            low, high = k * HD, k * HD + WINDOW
            for block in range(8):
                span = slice(block * ROWS, (block + 1) * ROWS)
                here = slice(block % 4 * ROWS, (block % 4 + 1) * ROWS)
                done = total_ref[span, low:high] + total[block // 4][here]
                out = outs[HOME.index((block // 4, (0, 1, 3, 2)[block % 4]))]
                out[:, low:high] = done.astype(jnp.bfloat16)
                if low:
                    out[:, :low] = total_ref[span, :low].astype(jnp.bfloat16)
                if high < WIDE:
                    out[:, high:] = total_ref[span, high:].astype(jnp.bfloat16)


def project(kernel, width, out_shape, places, whole, operands, where):
    vmem = pl.BlockSpec(memory_space=pltpu.VMEM)
    return pl.pallas_call(
        functools.partial(kernel, where),
        in_specs=[pl.BlockSpec(memory_space=pltpu.SMEM)] + [vmem] * (len(operands) + 1),
        out_specs=jax.tree.map(lambda _: vmem, out_shape),
        out_shape=out_shape,
        scratch_shapes=[pltpu.VMEM((width, D), jnp.bfloat16)],
        compiler_params=pltpu.CompilerParams(vmem_limit_bytes=PROJECT_VMEM),
        cost_estimate=pl.CostEstimate(flops=1, bytes_accessed=1, transcendentals=0),
        name=kernel.__name__.removesuffix("_kernel"),
    )(places, whole, *operands)


def attend_kernel(group_ref, length_ref, cos_ref, sin_ref, cache, *refs):
    blocks, out_ref, qkv, scores = refs[:8], *refs[8:]
    for i, block in enumerate(blocks):
        qkv[group_ref[i]] = block[...]
    scale = HD ** (-0.5) * LOG2E
    key_at = lax.broadcasted_iota(jnp.int32, (1, CAP), 1)
    token = lax.broadcasted_iota(jnp.int32, (GROUP * STRETCH, STRETCH), 0) % STRETCH
    causal = lax.broadcasted_iota(jnp.int32, (GROUP * STRETCH, STRETCH), 1) <= token

    def head(slot, h):
        low = (h % HEADS) * HD
        rows = slice(slot * STRETCH, (slot + 1) * STRETCH)
        return qkv[h // HEADS, rows, low : low + HD]

    def rotated(slot, h):
        rows = slice(slot * STRETCH, (slot + 1) * STRETCH)
        u = head(slot, h).astype(jnp.float32)
        turned = pltpu.roll(u, HD // 2, 1) * sin_ref[rows, :]
        return (u * cos_ref[rows, :] + turned).astype(jnp.bfloat16)

    def score(slot, k):
        hidden = jnp.where(key_at < length_ref[slot], 0.0, -jnp.inf)
        queries = [rotated(slot, k * GROUP + g) for g in range(GROUP)]
        queries = jnp.concatenate(queries, axis=0)
        new = lax.dot_general(
            queries, rotated(slot, HQ + k), NT, preferred_element_type=jnp.float32
        )
        new = jnp.where(causal, new, -jnp.inf)
        highest = None
        for low in range(0, CAP, CHUNK):
            keys = cache[slot, low : low + CHUNK, k * HD : (k + 1) * HD]
            part = lax.dot_general(
                queries, keys, NT, preferred_element_type=jnp.float32
            )
            part = part + hidden[:, low : low + CHUNK]
            scores[k % 2, :, low : low + CHUNK] = part
            part = jnp.maximum(part[:, :HD], part[:, HD:])
            highest = part if highest is None else jnp.maximum(highest, part)
        top = jnp.maximum(
            jnp.max(highest, axis=1, keepdims=True), jnp.max(new, axis=1, keepdims=True)
        )
        return top * scale, new

    def mix(slot, k, base, new):
        new = jnp.exp2(new * scale - base)
        mixed = jnp.dot(
            new.astype(jnp.bfloat16),
            head(slot, HQ + KVH + k),
            preferred_element_type=jnp.float32,
        )
        total = None
        for low in range(0, CAP, CHUNK):
            part = jnp.exp2(scores[k % 2, :, low : low + CHUNK] * scale - base)
            values = cache[slot, low : low + CHUNK, (KVH + k) * HD : (KVH + k + 1) * HD]
            mixed = mixed + jnp.dot(
                part.astype(jnp.bfloat16), values, preferred_element_type=jnp.float32
            )
            part = part[:, :HD] + part[:, HD:]
            total = part if total is None else total + part
        total = jnp.sum(total, axis=1, keepdims=True) + jnp.sum(
            new, axis=1, keepdims=True
        )
        mixed = (mixed / total).astype(jnp.bfloat16)
        for g in range(GROUP):
            low = (k * GROUP + g) * HD
            out_ref[slot * STRETCH : (slot + 1) * STRETCH, low : low + HD] = mixed[
                g * STRETCH : (g + 1) * STRETCH
            ]

    pairs = [(slot, k) for slot in range(SLOTS) for k in range(KVH)]
    ahead = None
    for pair in pairs:
        state = score(*pair)
        if ahead is not None:
            mix(*ahead)
        ahead = (*pair, *state)
    mix(*ahead)


def attend(groups, lengths, cosine, sine, cache, blocks):
    return pl.pallas_call(
        attend_kernel,
        in_specs=[pl.BlockSpec(memory_space=pltpu.SMEM)] * 2
        + [pl.BlockSpec(memory_space=pltpu.VMEM)] * 11,
        out_specs=pl.BlockSpec(memory_space=pltpu.VMEM),
        out_shape=jax.ShapeDtypeStruct((ROWS, HQ * HD), jnp.bfloat16),
        scratch_shapes=[
            pltpu.VMEM((8, ROWS, WIDE), jnp.bfloat16),
            pltpu.VMEM((2, GROUP * STRETCH, CAP), jnp.float32),
        ],
        compiler_params=pltpu.CompilerParams(vmem_limit_bytes=ATTEND_VMEM),
        name="attend",
    )(groups, lengths, cosine, sine, cache, *blocks)


def on_device(tokens, weight, bias, cache, lengths, slot_stream):
    t = lax.axis_index("tp")
    z = lax.axis_index("z")
    y = lax.axis_index("y")
    xl = lax.axis_index("xl")
    group = t * 4 + z
    index = (group * 4 + y) * 2 + xl

    own = weight.T
    own_side, three, one = shift(own, dx=1), shift(own, dy=3), shift(own, dy=1)
    early = shift(jnp.zeros((16, HD), jnp.bfloat16), dt=1)
    late = copy_rows(tokens, early)
    late, bias, lengths, slot_stream = lax.optimization_barrier(
        (late, bias, lengths, slot_stream)
    )

    far_y = (y + 2) % 4
    places = []
    for dy in range(4):
        base = far_y * 2 * STRETCH if dy == 2 else (y - dy) % 4 * 2 * COLS
        places += [base + xl * COLS, base + (1 - xl) * COLS]
    places += [far_y * 2 * COLS, far_y * 2 * STRETCH]
    places = jnp.stack(places).astype(jnp.int32)
    groups = [(t + dt) % 2 * 4 + (z + dz) % 4 for dt, dz in HOME]
    groups = jnp.stack(groups).astype(jnp.int32)
    bias_cols = lax.dynamic_slice_in_dim(bias, group * WIDE, WIDE, 0)
    bias_cols = bias_cols.astype(jnp.float32)[None, :]

    my_slots = index * SLOTS + jnp.arange(SLOTS, dtype=jnp.int32)
    my_lengths = jnp.take(lengths, jnp.take(slot_stream, my_slots)).astype(jnp.int32)
    positions = (my_lengths[:, None] + jnp.arange(STRETCH, dtype=jnp.int32)).reshape(-1)
    frequency = ROPE_THETA ** (
        -(jnp.arange(HD // 2, dtype=jnp.float32) * 2.0) / HD
    )
    angles = positions.astype(jnp.float32)[:, None] * frequency[None, :]
    cosine, sine = jnp.cos(angles), jnp.sin(angles)
    cosine = jnp.concatenate([cosine, cosine], axis=1)
    sine = jnp.concatenate([-sine, sine], axis=1)

    up, down = shift(late, dz=1), shift(late, dz=3)
    own_side, tokens, late, small = lax.optimization_barrier(
        (own_side, tokens, late, (places, groups, bias_cols, my_lengths, cosine, sine))
    )
    places, groups, bias_cols, my_lengths, cosine, sine = small
    far = shift(late, dz=2)
    one_side, three_side = shift(one, dx=3), shift(three, dx=1)
    two_side = shift(own_side, dy=2)
    near = jnp.concatenate([tokens, up, down])
    low, high = one[:, :HALF], three[:, HALF:]
    two_side, one_side, three_side, far, near = lax.optimization_barrier(
        (two_side, one_side, three_side, far, near)
    )
    two_low, two_high = shift(low, dy=1), shift(high, dy=3)
    other = shift(near, dt=1)
    other_far = shift(far, dt=1)

    total, rows = project(
        project_first_kernel,
        WIDE,
        [
            jax.ShapeDtypeStruct((2 * NEAR, WIDE), jnp.float32),
            jax.ShapeDtypeStruct((2 * NEAR, D), jnp.bfloat16),
        ],
        places,
        bias_cols,
        [own, own_side, one, one_side, three, three_side, near, far, other, other_far],
        tuple((place, 0) for place in (0, 1, 2, 3, 6, 7)),
    )
    parts = project(
        project_last_kernel,
        WINDOW,
        [jax.ShapeDtypeStruct((ROWS, WIDE), jnp.bfloat16)] * 8,
        places,
        total,
        [two_low, two_high, two_side, rows],
        ((4, 0), (4, HALF), (5, 0)),
    )
    blocks = [
        shift(part, dt=-dt, dz=-dz) if dt or dz else part
        for part, (dt, dz) in zip(parts, HOME)
    ]
    return attend(groups, my_lengths, cosine, sine, cache, blocks)


def solution(mesh):
    fine = Mesh(mesh.devices.reshape(2, 4, 4, 2, 2), AXES)
    part = ("xh", "tp", "z", "y", "xl")
    in_specs = (
        P(part, None),
        P(None, ("tp", "z", "y", "xl")),
        P(),
        P(part, None, None),
        P("xh"),
        P("xh"),
    )
    return jax.shard_map(
        on_device,
        mesh=fine,
        in_specs=in_specs,
        out_specs=P(part, None),
        check_vma=False,
    )
```

```python
import functools

import jax
import jax.numpy as jnp
from jax import lax
from jax.experimental import pallas as pl
from jax.experimental.pallas import tpu as pltpu
from jax.sharding import Mesh, PartitionSpec as P

D = 4096
HD = 128
HQ = 32
KVH = 4
STRETCH = 16
CAP = 1024
GROUP = 8
SLOTS = 4
ROWS = SLOTS * STRETCH
COLS = 80
SHARDS = 8
WIDE = COLS * SHARDS
HEADS = WIDE // HD
HALF = D // 2
ROPE_THETA = 1000000.0
LOG2E = 1.4426950408889634
AXES = ("tp", "z", "y", "xl", "xh")
NEAR = 4 * ROWS
WINDOW = 256
CHUNK = 256
PROJECT_VMEM = 14 * 1024 * 1024
ATTEND_VMEM = 8 * 1024 * 1024
NT = (((1,), (1,)), ((), ()))
HOME = [(0, 2), (1, 2), (0, 1), (1, 1), (0, 3), (1, 3), (1, 0), (0, 0)]


def device_index(t, z, y, x):
    x = x % 4
    return ((((t % 2) * 4 + z % 4) * 4 + y % 4) * 2 + x % 2) * 2 + x // 2


def shift(array, dt=0, dz=0, dy=0, dx=0):
    pairs = [
        (device_index(t, z, y, x), device_index(t + dt, z + dz, y + dy, x + dx))
        for t in range(2)
        for z in range(4)
        for y in range(4)
        for x in range(4)
    ]
    return lax.ppermute(array, AXES, pairs)


def copy_rows_kernel(rows, early, out, sem):
    copy = pltpu.make_async_copy(rows, out, sem)
    copy.start()
    copy.wait()


def copy_rows(rows, early):
    return pl.pallas_call(
        copy_rows_kernel,
        in_specs=[pl.BlockSpec(memory_space=pltpu.HBM), pl.BlockSpec(memory_space=pl.ANY)],
        out_specs=pl.BlockSpec(memory_space=pltpu.VMEM),
        out_shape=jax.ShapeDtypeStruct((ROWS, D), jnp.bfloat16),
        scratch_shapes=[pltpu.SemaphoreType.DMA],
        compiler_params=pltpu.CompilerParams(vmem_limit_bytes=8 * 1024 * 1024),
        name="copy_rows",
    )(rows, early)


def gather(pieces, where, at_ref, weights):
    for piece, (place, low) in zip(pieces, where):
        start = pl.multiple_of(at_ref[place], 16)
        weights[pl.ds(start, COLS), low : low + piece.shape[1]] = piece[...]


def multiply(rows, weights):
    return [
        lax.dot_general(
            rows[low : low + NEAR, :],
            weights[...],
            NT,
            preferred_element_type=jnp.float32,
        )
        for low in (0, NEAR)
    ]


def project_first_kernel(where, at_ref, bias_ref, *refs):
    pieces, blocks = refs[:-7], refs[-7:-3]
    out, rows, weights = refs[-3:]
    start = pl.multiple_of(at_ref[8], 16)
    weights[pl.ds(start, 2 * COLS), :] = jnp.zeros((2 * COLS, D), jnp.bfloat16)
    gather(pieces, where, at_ref, weights)
    low = 0
    for block in blocks:
        rows[low : low + block.shape[0], :] = block[...]
        low += block.shape[0]
    first, second = multiply(rows, weights)
    out[:NEAR] = first + bias_ref[...]
    out[NEAR:] = second + bias_ref[...]


def project_last_kernel(where, at_ref, total_ref, *refs):
    pieces, rows = refs[:-10], refs[-10]
    outs, weights = refs[-9:-1], refs[-1]
    shift_by = at_ref[9]
    for k in range(4):

        @pl.when(shift_by == 2 * k * STRETCH)
        def _():
            low, high = 2 * k * STRETCH, 2 * k * STRETCH + 2 * COLS
            if low:
                weights[:low, :] = jnp.zeros((low, D), jnp.bfloat16)
            if high < WINDOW:
                weights[high:, :] = jnp.zeros((WINDOW - high, D), jnp.bfloat16)

    gather(pieces, where, at_ref, weights)
    total = multiply(rows, weights)
    for k in range(4):

        @pl.when(shift_by == 2 * k * STRETCH)
        def _():
            low, high = k * HD, k * HD + WINDOW
            for block in range(8):
                span = slice(block * ROWS, (block + 1) * ROWS)
                here = slice(block % 4 * ROWS, (block % 4 + 1) * ROWS)
                done = total_ref[span, low:high] + total[block // 4][here]
                out = outs[HOME.index((block // 4, (0, 1, 3, 2)[block % 4]))]
                out[:, low:high] = done.astype(jnp.bfloat16)
                if low:
                    out[:, :low] = total_ref[span, :low].astype(jnp.bfloat16)
                if high < WIDE:
                    out[:, high:] = total_ref[span, high:].astype(jnp.bfloat16)


def project(kernel, width, out_shape, places, whole, operands, where):
    vmem = pl.BlockSpec(memory_space=pltpu.VMEM)
    return pl.pallas_call(
        functools.partial(kernel, where),
        in_specs=[pl.BlockSpec(memory_space=pltpu.SMEM)] + [vmem] * (len(operands) + 1),
        out_specs=jax.tree.map(lambda _: vmem, out_shape),
        out_shape=out_shape,
        scratch_shapes=[pltpu.VMEM((width, D), jnp.bfloat16)],
        compiler_params=pltpu.CompilerParams(vmem_limit_bytes=PROJECT_VMEM),
        cost_estimate=pl.CostEstimate(flops=1, bytes_accessed=1, transcendentals=0),
        name=kernel.__name__.removesuffix("_kernel"),
    )(places, whole, *operands)


def attend_kernel(group_ref, length_ref, cos_ref, sin_ref, cache, *refs):
    blocks, out_ref, qkv, scores = refs[:8], *refs[8:]
    for i, block in enumerate(blocks):
        qkv[group_ref[i]] = block[...]
    scale = HD ** (-0.5) * LOG2E
    key_at = lax.broadcasted_iota(jnp.int32, (1, CAP), 1)
    token = lax.broadcasted_iota(jnp.int32, (GROUP * STRETCH, STRETCH), 0) % STRETCH
    causal = lax.broadcasted_iota(jnp.int32, (GROUP * STRETCH, STRETCH), 1) <= token

    def head(slot, h):
        low = (h % HEADS) * HD
        rows = slice(slot * STRETCH, (slot + 1) * STRETCH)
        return qkv[h // HEADS, rows, low : low + HD]

    def rotated(slot, h):
        rows = slice(slot * STRETCH, (slot + 1) * STRETCH)
        u = head(slot, h).astype(jnp.float32)
        turned = pltpu.roll(u, HD // 2, 1) * sin_ref[rows, :]
        return (u * cos_ref[rows, :] + turned).astype(jnp.bfloat16)

    def score(slot, k):
        hidden = jnp.where(key_at < length_ref[slot], 0.0, -jnp.inf)
        queries = [rotated(slot, k * GROUP + g) for g in range(GROUP)]
        queries = jnp.concatenate(queries, axis=0)
        new = lax.dot_general(
            queries, rotated(slot, HQ + k), NT, preferred_element_type=jnp.float32
        )
        new = jnp.where(causal, new, -jnp.inf)
        highest = None
        for low in range(0, CAP, CHUNK):
            keys = cache[slot, low : low + CHUNK, k * HD : (k + 1) * HD]
            part = lax.dot_general(
                queries, keys, NT, preferred_element_type=jnp.float32
            )
            part = part + hidden[:, low : low + CHUNK]
            scores[k % 2, :, low : low + CHUNK] = part
            part = jnp.maximum(part[:, :HD], part[:, HD:])
            highest = part if highest is None else jnp.maximum(highest, part)
        top = jnp.maximum(
            jnp.max(highest, axis=1, keepdims=True), jnp.max(new, axis=1, keepdims=True)
        )
        return top, new

    def mix(slot, k, top, new):
        new = jnp.exp2((new - top) * scale)
        mixed = jnp.dot(
            new.astype(jnp.bfloat16),
            head(slot, HQ + KVH + k),
            preferred_element_type=jnp.float32,
        )
        total = None
        for low in range(0, CAP, CHUNK):
            part = jnp.exp2((scores[k % 2, :, low : low + CHUNK] - top) * scale)
            values = cache[slot, low : low + CHUNK, (KVH + k) * HD : (KVH + k + 1) * HD]
            mixed = mixed + jnp.dot(
                part.astype(jnp.bfloat16), values, preferred_element_type=jnp.float32
            )
            part = part[:, :HD] + part[:, HD:]
            total = part if total is None else total + part
        total = jnp.sum(total, axis=1, keepdims=True) + jnp.sum(
            new, axis=1, keepdims=True
        )
        mixed = (mixed / total).astype(jnp.bfloat16)
        for g in range(GROUP):
            low = (k * GROUP + g) * HD
            out_ref[slot * STRETCH : (slot + 1) * STRETCH, low : low + HD] = mixed[
                g * STRETCH : (g + 1) * STRETCH
            ]

    pairs = [(slot, k) for slot in range(SLOTS) for k in range(KVH)]
    ahead = None
    for pair in pairs:
        state = score(*pair)
        if ahead is not None:
            mix(*ahead)
        ahead = (*pair, *state)
    mix(*ahead)


def attend(groups, lengths, cosine, sine, cache, blocks):
    return pl.pallas_call(
        attend_kernel,
        in_specs=[pl.BlockSpec(memory_space=pltpu.SMEM)] * 2
        + [pl.BlockSpec(memory_space=pltpu.VMEM)] * 11,
        out_specs=pl.BlockSpec(memory_space=pltpu.VMEM),
        out_shape=jax.ShapeDtypeStruct((ROWS, HQ * HD), jnp.bfloat16),
        scratch_shapes=[
            pltpu.VMEM((8, ROWS, WIDE), jnp.bfloat16),
            pltpu.VMEM((2, GROUP * STRETCH, CAP), jnp.float32),
        ],
        compiler_params=pltpu.CompilerParams(vmem_limit_bytes=ATTEND_VMEM),
        name="attend",
    )(groups, lengths, cosine, sine, cache, *blocks)


def on_device(tokens, weight, bias, cache, lengths, slot_stream):
    t = lax.axis_index("tp")
    z = lax.axis_index("z")
    y = lax.axis_index("y")
    xl = lax.axis_index("xl")
    group = t * 4 + z
    index = (group * 4 + y) * 2 + xl

    own = weight.T
    own_side, three, one = shift(own, dx=1), shift(own, dy=3), shift(own, dy=1)
    early = shift(jnp.zeros((16, HD), jnp.bfloat16), dt=1)
    late = copy_rows(tokens, early)
    late, bias, lengths, slot_stream = lax.optimization_barrier(
        (late, bias, lengths, slot_stream)
    )

    far_y = (y + 2) % 4
    places = []
    for dy in range(4):
        base = far_y * 2 * STRETCH if dy == 2 else (y - dy) % 4 * 2 * COLS
        places += [base + xl * COLS, base + (1 - xl) * COLS]
    places += [far_y * 2 * COLS, far_y * 2 * STRETCH]
    places = jnp.stack(places).astype(jnp.int32)
    groups = [(t + dt) % 2 * 4 + (z + dz) % 4 for dt, dz in HOME]
    groups = jnp.stack(groups).astype(jnp.int32)
    bias_cols = lax.dynamic_slice_in_dim(bias, group * WIDE, WIDE, 0)
    bias_cols = bias_cols.astype(jnp.float32)[None, :]

    my_slots = index * SLOTS + jnp.arange(SLOTS, dtype=jnp.int32)
    my_lengths = jnp.take(lengths, jnp.take(slot_stream, my_slots)).astype(jnp.int32)
    positions = (my_lengths[:, None] + jnp.arange(STRETCH, dtype=jnp.int32)).reshape(-1)
    frequency = ROPE_THETA ** (
        -(jnp.arange(HD // 2, dtype=jnp.float32) * 2.0) / HD
    )
    angles = positions.astype(jnp.float32)[:, None] * frequency[None, :]
    cosine, sine = jnp.cos(angles), jnp.sin(angles)
    cosine = jnp.concatenate([cosine, cosine], axis=1)
    sine = jnp.concatenate([-sine, sine], axis=1)

    up, down = shift(late, dz=1), shift(late, dz=3)
    own_side, tokens, late, small = lax.optimization_barrier(
        (own_side, tokens, late, (places, groups, bias_cols, my_lengths, cosine, sine))
    )
    places, groups, bias_cols, my_lengths, cosine, sine = small
    far = shift(late, dz=2)
    one_side, three_side = shift(one, dx=3), shift(three, dx=1)
    two_side = shift(own_side, dy=2)
    near = jnp.concatenate([tokens, up, down])
    low, high = one[:, :HALF], three[:, HALF:]
    two_side, one_side, three_side, far, near = lax.optimization_barrier(
        (two_side, one_side, three_side, far, near)
    )
    two_low, two_high = shift(low, dy=1), shift(high, dy=3)
    other = shift(near, dt=1)
    other_far = shift(far, dt=1)

    total, rows = project(
        project_first_kernel,
        WIDE,
        [
            jax.ShapeDtypeStruct((2 * NEAR, WIDE), jnp.float32),
            jax.ShapeDtypeStruct((2 * NEAR, D), jnp.bfloat16),
        ],
        places,
        bias_cols,
        [own, own_side, one, one_side, three, three_side, near, far, other, other_far],
        tuple((place, 0) for place in (0, 1, 2, 3, 6, 7)),
    )
    parts = project(
        project_last_kernel,
        WINDOW,
        [jax.ShapeDtypeStruct((ROWS, WIDE), jnp.bfloat16)] * 8,
        places,
        total,
        [two_low, two_high, two_side, rows],
        ((4, 0), (4, HALF), (5, 0)),
    )
    blocks = [
        shift(part, dt=-dt, dz=-dz) if dt or dz else part
        for part, (dt, dz) in zip(parts, HOME)
    ]
    return attend(groups, my_lengths, cosine, sine, cache, blocks)


def solution(mesh):
    fine = Mesh(mesh.devices.reshape(2, 4, 4, 2, 2), AXES)
    part = ("xh", "tp", "z", "y", "xl")
    in_specs = (
        P(part, None),
        P(None, ("tp", "z", "y", "xl")),
        P(),
        P(part, None, None),
        P("xh"),
        P("xh"),
    )
    return jax.shard_map(
        on_device,
        mesh=fine,
        in_specs=in_specs,
        out_specs=P(part, None),
        check_vma=False,
    )
```

```python
import functools

import jax
import jax.numpy as jnp
from jax import lax
from jax.experimental import pallas as pl
from jax.experimental.pallas import tpu as pltpu
from jax.sharding import Mesh, PartitionSpec as P

D = 4096
HD = 128
HQ = 32
KVH = 4
STRETCH = 16
CAP = 1024
GROUP = 8
SLOTS = 4
ROWS = SLOTS * STRETCH
COLS = 80
SHARDS = 8
WIDE = COLS * SHARDS
HEADS = WIDE // HD
HALF = D // 2
ROPE_THETA = 1000000.0
LOG2E = 1.4426950408889634
AXES = ("tp", "z", "y", "xl", "xh")
NEAR = 4 * ROWS
WINDOW = 256
CHUNK = 256
PROJECT_VMEM = 14 * 1024 * 1024
ATTEND_VMEM = 8 * 1024 * 1024
NT = (((1,), (1,)), ((), ()))
HOME = [(0, 2), (1, 2), (0, 1), (1, 1), (0, 3), (1, 3), (1, 0), (0, 0)]


def device_index(t, z, y, x):
    x = x % 4
    return ((((t % 2) * 4 + z % 4) * 4 + y % 4) * 2 + x % 2) * 2 + x // 2


def shift(array, dt=0, dz=0, dy=0, dx=0):
    pairs = [
        (device_index(t, z, y, x), device_index(t + dt, z + dz, y + dy, x + dx))
        for t in range(2)
        for z in range(4)
        for y in range(4)
        for x in range(4)
    ]
    return lax.ppermute(array, AXES, pairs)


def copy_rows_kernel(rows, early, out, sem):
    copy = pltpu.make_async_copy(rows, out, sem)
    copy.start()
    copy.wait()


def copy_rows(rows, early):
    return pl.pallas_call(
        copy_rows_kernel,
        in_specs=[pl.BlockSpec(memory_space=pltpu.HBM), pl.BlockSpec(memory_space=pl.ANY)],
        out_specs=pl.BlockSpec(memory_space=pltpu.VMEM),
        out_shape=jax.ShapeDtypeStruct((ROWS, D), jnp.bfloat16),
        scratch_shapes=[pltpu.SemaphoreType.DMA],
        compiler_params=pltpu.CompilerParams(vmem_limit_bytes=8 * 1024 * 1024),
        name="copy_rows",
    )(rows, early)


def gather(pieces, where, at_ref, weights):
    for piece, (place, low) in zip(pieces, where):
        start = pl.multiple_of(at_ref[place], 16)
        weights[pl.ds(start, COLS), low : low + piece.shape[1]] = piece[...]


def multiply(rows, weights):
    return [
        lax.dot_general(
            rows[low : low + NEAR, :],
            weights[...],
            NT,
            preferred_element_type=jnp.float32,
        )
        for low in (0, NEAR)
    ]


def project_first_kernel(where, at_ref, bias_ref, *refs):
    pieces, blocks = refs[:-7], refs[-7:-3]
    out, rows, weights = refs[-3:]
    start = pl.multiple_of(at_ref[8], 16)
    weights[pl.ds(start, 2 * COLS), :] = jnp.zeros((2 * COLS, D), jnp.bfloat16)
    gather(pieces, where, at_ref, weights)
    low = 0
    for block in blocks:
        rows[low : low + block.shape[0], :] = block[...]
        low += block.shape[0]
    first, second = multiply(rows, weights)
    out[:NEAR] = first + bias_ref[...]
    out[NEAR:] = second + bias_ref[...]


def project_last_kernel(where, at_ref, total_ref, *refs):
    pieces, rows = refs[:-10], refs[-10]
    outs, weights = refs[-9:-1], refs[-1]
    shift_by = at_ref[9]
    for k in range(4):

        @pl.when(shift_by == 2 * k * STRETCH)
        def _():
            low, high = 2 * k * STRETCH, 2 * k * STRETCH + 2 * COLS
            if low:
                weights[:low, :] = jnp.zeros((low, D), jnp.bfloat16)
            if high < WINDOW:
                weights[high:, :] = jnp.zeros((WINDOW - high, D), jnp.bfloat16)

    gather(pieces, where, at_ref, weights)
    total = multiply(rows, weights)
    for k in range(4):

        @pl.when(shift_by == 2 * k * STRETCH)
        def _():
            low, high = k * HD, k * HD + WINDOW
            for block in range(8):
                span = slice(block * ROWS, (block + 1) * ROWS)
                here = slice(block % 4 * ROWS, (block % 4 + 1) * ROWS)
                done = total_ref[span, low:high] + total[block // 4][here]
                out = outs[HOME.index((block // 4, (0, 1, 3, 2)[block % 4]))]
                out[:, low:high] = done.astype(jnp.bfloat16)
                if low:
                    out[:, :low] = total_ref[span, :low].astype(jnp.bfloat16)
                if high < WIDE:
                    out[:, high:] = total_ref[span, high:].astype(jnp.bfloat16)


def project(kernel, width, out_shape, places, whole, operands, where):
    vmem = pl.BlockSpec(memory_space=pltpu.VMEM)
    return pl.pallas_call(
        functools.partial(kernel, where),
        in_specs=[pl.BlockSpec(memory_space=pltpu.SMEM)] + [vmem] * (len(operands) + 1),
        out_specs=jax.tree.map(lambda _: vmem, out_shape),
        out_shape=out_shape,
        scratch_shapes=[pltpu.VMEM((width, D), jnp.bfloat16)],
        compiler_params=pltpu.CompilerParams(vmem_limit_bytes=PROJECT_VMEM),
        cost_estimate=pl.CostEstimate(flops=1, bytes_accessed=1, transcendentals=0),
        name=kernel.__name__.removesuffix("_kernel"),
    )(places, whole, *operands)


def attend_kernel(group_ref, length_ref, cos_ref, sin_ref, cache, *refs):
    blocks, out_ref, qkv, scores = refs[:8], *refs[8:]
    for i, block in enumerate(blocks):
        qkv[group_ref[i]] = block[...]
    scale = HD ** (-0.5) * LOG2E
    key_at = lax.broadcasted_iota(jnp.int32, (1, CAP), 1)
    token = lax.broadcasted_iota(jnp.int32, (GROUP * STRETCH, STRETCH), 0) % STRETCH
    causal = lax.broadcasted_iota(jnp.int32, (GROUP * STRETCH, STRETCH), 1) <= token

    def head(slot, h):
        low = (h % HEADS) * HD
        rows = slice(slot * STRETCH, (slot + 1) * STRETCH)
        return qkv[h // HEADS, rows, low : low + HD]

    def rotated(slot, h):
        rows = slice(slot * STRETCH, (slot + 1) * STRETCH)
        u = head(slot, h).astype(jnp.float32)
        turned = pltpu.roll(u, HD // 2, 1) * sin_ref[rows, :]
        return (u * cos_ref[rows, :] + turned).astype(jnp.bfloat16)

    def score(slot, k):
        hidden = jnp.where(key_at < length_ref[slot], 0.0, -jnp.inf)
        queries = [rotated(slot, k * GROUP + g) for g in range(GROUP)]
        queries = jnp.concatenate(queries, axis=0)
        new = lax.dot_general(
            queries, rotated(slot, HQ + k), NT, preferred_element_type=jnp.float32
        )
        new = jnp.where(causal, new, -jnp.inf)
        highest = None
        for low in range(0, CAP, CHUNK):
            keys = cache[slot, low : low + CHUNK, k * HD : (k + 1) * HD]
            part = lax.dot_general(
                queries, keys, NT, preferred_element_type=jnp.float32
            )
            part = part + hidden[:, low : low + CHUNK]
            scores[k % 2, :, low : low + CHUNK] = part
            part = jnp.maximum(part[:, :HD], part[:, HD:])
            highest = part if highest is None else jnp.maximum(highest, part)
        top = jnp.maximum(
            jnp.max(highest, axis=1, keepdims=True), jnp.max(new, axis=1, keepdims=True)
        )
        return top, new

    def mix(slot, k, top, new):
        new = jnp.exp2((new - top) * scale)
        mixed = jnp.dot(
            new.astype(jnp.bfloat16),
            head(slot, HQ + KVH + k),
            preferred_element_type=jnp.float32,
        )
        total = None
        for low in range(0, CAP, CHUNK):
            part = jnp.exp2((scores[k % 2, :, low : low + CHUNK] - top) * scale)
            values = cache[slot, low : low + CHUNK, (KVH + k) * HD : (KVH + k + 1) * HD]
            mixed = mixed + jnp.dot(
                part.astype(jnp.bfloat16), values, preferred_element_type=jnp.float32
            )
            part = part[:, :HD] + part[:, HD:]
            total = part if total is None else total + part
        total = jnp.sum(total, axis=1, keepdims=True) + jnp.sum(
            new, axis=1, keepdims=True
        )
        mixed = (mixed / total).astype(jnp.bfloat16)
        for g in range(GROUP):
            low = (k * GROUP + g) * HD
            out_ref[slot * STRETCH : (slot + 1) * STRETCH, low : low + HD] = mixed[
                g * STRETCH : (g + 1) * STRETCH
            ]

    pairs = [(slot, k) for slot in range(SLOTS) for k in range(KVH)]
    ahead = None
    for pair in pairs:
        state = score(*pair)
        if ahead is not None:
            mix(*ahead)
        ahead = (*pair, *state)
    mix(*ahead)


def attend(groups, lengths, cosine, sine, cache, blocks):
    return pl.pallas_call(
        attend_kernel,
        in_specs=[pl.BlockSpec(memory_space=pltpu.SMEM)] * 2
        + [pl.BlockSpec(memory_space=pltpu.VMEM)] * 11,
        out_specs=pl.BlockSpec(memory_space=pltpu.VMEM),
        out_shape=jax.ShapeDtypeStruct((ROWS, HQ * HD), jnp.bfloat16),
        scratch_shapes=[
            pltpu.VMEM((8, ROWS, WIDE), jnp.bfloat16),
            pltpu.VMEM((2, GROUP * STRETCH, CAP), jnp.float32),
        ],
        compiler_params=pltpu.CompilerParams(vmem_limit_bytes=ATTEND_VMEM),
        name="attend",
    )(groups, lengths, cosine, sine, cache, *blocks)


def on_device(tokens, weight, bias, cache, lengths, slot_stream):
    t = lax.axis_index("tp")
    z = lax.axis_index("z")
    y = lax.axis_index("y")
    xl = lax.axis_index("xl")
    group = t * 4 + z
    index = (group * 4 + y) * 2 + xl

    own = weight.T
    own_side, three, one = shift(own, dx=1), shift(own, dy=3), shift(own, dy=1)
    early = shift(jnp.zeros((16, HD), jnp.bfloat16), dt=1)
    late = copy_rows(tokens, early)
    late, bias, lengths, slot_stream = lax.optimization_barrier(
        (late, bias, lengths, slot_stream)
    )

    far_y = (y + 2) % 4
    places = []
    for dy in range(4):
        base = far_y * 2 * STRETCH if dy == 2 else (y - dy) % 4 * 2 * COLS
        places += [base + xl * COLS, base + (1 - xl) * COLS]
    places += [far_y * 2 * COLS, far_y * 2 * STRETCH]
    places = jnp.stack(places).astype(jnp.int32)
    groups = [(t + dt) % 2 * 4 + (z + dz) % 4 for dt, dz in HOME]
    groups = jnp.stack(groups).astype(jnp.int32)
    bias_cols = lax.dynamic_slice_in_dim(bias, group * WIDE, WIDE, 0)
    bias_cols = bias_cols.astype(jnp.float32)[None, :]

    my_slots = index * SLOTS + jnp.arange(SLOTS, dtype=jnp.int32)
    my_lengths = jnp.take(lengths, jnp.take(slot_stream, my_slots)).astype(jnp.int32)
    positions = (my_lengths[:, None] + jnp.arange(STRETCH, dtype=jnp.int32)).reshape(-1)
    frequency = ROPE_THETA ** (
        -(jnp.arange(HD // 2, dtype=jnp.float32) * 2.0) / HD
    )
    angles = positions.astype(jnp.float32)[:, None] * frequency[None, :]
    cosine, sine = jnp.cos(angles), jnp.sin(angles)
    cosine = jnp.concatenate([cosine, cosine], axis=1)
    sine = jnp.concatenate([-sine, sine], axis=1)

    up, down = shift(late, dz=1), shift(late, dz=3)
    one, tokens, late, small = lax.optimization_barrier(
        (one, tokens, late, (places, groups, bias_cols, my_lengths, cosine, sine))
    )
    places, groups, bias_cols, my_lengths, cosine, sine = small
    far = shift(late, dz=2)
    one_side, three_side = shift(one, dx=3), shift(three, dx=1)
    two_side = shift(own_side, dy=2)
    near = jnp.concatenate([tokens, up, down])
    low, high = one[:, :HALF], three[:, HALF:]
    two_side, one_side, three_side, far, near = lax.optimization_barrier(
        (two_side, one_side, three_side, far, near)
    )
    two_low, two_high = shift(low, dy=1), shift(high, dy=3)
    other = shift(near, dt=1)
    other_far = shift(far, dt=1)

    total, rows = project(
        project_first_kernel,
        WIDE,
        [
            jax.ShapeDtypeStruct((2 * NEAR, WIDE), jnp.float32),
            jax.ShapeDtypeStruct((2 * NEAR, D), jnp.bfloat16),
        ],
        places,
        bias_cols,
        [own, own_side, one, one_side, three, three_side, near, far, other, other_far],
        tuple((place, 0) for place in (0, 1, 2, 3, 6, 7)),
    )
    parts = project(
        project_last_kernel,
        WINDOW,
        [jax.ShapeDtypeStruct((ROWS, WIDE), jnp.bfloat16)] * 8,
        places,
        total,
        [two_low, two_high, two_side, rows],
        ((4, 0), (4, HALF), (5, 0)),
    )
    blocks = [
        shift(part, dt=-dt, dz=-dz) if dt or dz else part
        for part, (dt, dz) in zip(parts, HOME)
    ]
    return attend(groups, my_lengths, cosine, sine, cache, blocks)


def solution(mesh):
    fine = Mesh(mesh.devices.reshape(2, 4, 4, 2, 2), AXES)
    part = ("xh", "tp", "z", "y", "xl")
    in_specs = (
        P(part, None),
        P(None, ("tp", "z", "y", "xl")),
        P(),
        P(part, None, None),
        P("xh"),
        P("xh"),
    )
    return jax.shard_map(
        on_device,
        mesh=fine,
        in_specs=in_specs,
        out_specs=P(part, None),
        check_vma=False,
    )
```
